768 devices in a mesh: gz: 16 (over y, core), ta: 48 (over x, z).
Axes of the slice: x: 4, y: 8, z: 12, core: 2. Of those that a mesh axis runs over, the one named last changes fastest.
Arguments:
- coarse_vectors: float32 [16, 48, 1, 1, 256, 128], P('gz', 'ta'), may hold values from -120 to 120
- self_links: bfloat16 [16, 48, 1, 1, 128, 128], P('gz', 'ta'), may hold values from -0.306066 to 0.306066, as said below
- hop_links: bfloat16 [4, 16, 48, 1, 1, 128, 128], P(None, 'gz', 'ta'), may hold values from -0.026516504 to 0.026516504
- basis: bfloat16 [16, 48, 1, 1, 128, 9216], P('gz', 'ta'), may hold values from -0.5 to 0.5
- selected: int32 [32], replicated, may hold values from 0 to 255, as said below
Outputs:
- fine_vectors: bfloat16 [16, 48, 1, 1, 2, 32, 9216], P('gz', 'ta')
The draws below stay inside these ranges and needn't reach their ends.
Inputs may be any that keep to these rules, and one draw needn't show every extreme that they name: `self_links`: symmetric in its last two dimensions. `selected`: 32 distinct indices; 0 and 255 are always among them.
All inputs are finite; a program needn't handle non-finite values.
Results may differ from the reference program's by a relative error of at most 0.0065.
Values may be sent and summed in bfloat16 or wider, within the bound.
No kernel may reach another device: no remote copies, remote signals or barrier semaphores. Data moves between devices by JAX's collectives and lax.ppermute only.
A program may use at most 32 MiB of HBM per device.

```python
import jax
import jax.numpy as jnp
from jax import lax

BASIS = 64
FINE = 9216
NVEC = 256
KSEL = 32
DEG = 16
BX = 1
BY = 1
NZB = 16
NTB = 48


def log_uniform(key, shape, low, high):
    return jnp.exp(jax.random.uniform(key, shape, jnp.float32, jnp.log(low), jnp.log(high)))


def draw_coarse_vectors(key, part):
    key = jax.random.fold_in(key, 11)
    subkeys = jax.random.split(key, 3)
    width = 2 * BASIS
    shape = (NZB, NTB, BX, BY, NVEC, width)
    depth_share = jnp.arange(NZB, dtype=jnp.float32) / NZB
    time_share = jnp.arange(NTB, dtype=jnp.float32) / NTB
    rising = 3.0 ** (0.5 * depth_share[:, None] + 0.5 * time_share[None, :])
    rising = rising[:, :, None, None, None, None]
    column_scale = log_uniform(subkeys[0], (NVEC, 1), 1.0, 10.0)
    row_scale = log_uniform(subkeys[1], (NZB, NTB, BX, BY, 1, 1), 1.0, 10.0)
    random_part = jax.random.truncated_normal(subkeys[2], -4.0, 4.0, shape, jnp.float32)
    values = random_part * row_scale * column_scale * rising / 10.0
    return values


def draw_self_links(key, part):
    key = jax.random.fold_in(key, 12)
    subkeys = jax.random.split(key, 2)
    width = 2 * BASIS
    shape = (NZB, NTB, BX, BY, width, width)
    spread = 0.212 / width ** 0.5
    random_part = jax.random.truncated_normal(subkeys[0], -4.0, 4.0, shape, jnp.float32)
    symmetric = (random_part + jnp.swapaxes(random_part, -1, -2)) * (spread / 2.0 ** 0.5)
    diagonal_part = jax.random.uniform(subkeys[1], (NZB, NTB, BX, BY, width, 1), jnp.float32, -0.2, 0.2)
    identity = (jnp.arange(width)[:, None] == jnp.arange(width)[None, :]).astype(jnp.float32)
    return (symmetric + diagonal_part * identity).astype(jnp.bfloat16)


def draw_hop_links(key, part):
    key = jax.random.fold_in(key, 13)
    width = 2 * BASIS
    shape = (4, NZB, NTB, BX, BY, width, width)
    spread = 0.075 / width ** 0.5
    random_part = jax.random.truncated_normal(key, -4.0, 4.0, shape, jnp.float32)
    return (random_part * spread).astype(jnp.bfloat16)


def draw_selected(key, part):
    key = jax.random.fold_in(key, 14)
    subkeys = jax.random.split(key, 2)
    middle = jax.random.permutation(subkeys[0], NVEC - 2)[:KSEL - 2] + 1
    chosen = jnp.concatenate([jnp.array([0, NVEC - 1], dtype=jnp.int32), middle.astype(jnp.int32)])
    return chosen[jax.random.permutation(subkeys[1], KSEL)]


def block_levels(own_key, shape, cuts, least, high):
    def one(dim, parts):
        steps = jax.random.uniform(jax.random.fold_in(jax.random.fold_in(own_key, 6), dim), (parts,), jnp.float32, least / len(cuts), high / len(cuts))
        return jnp.repeat(jnp.exp(steps), shape[dim] // parts).reshape((-1,) + (1,) * (len(shape) - dim - 1))

    factor_of = one(*cuts[0])
    for cut in cuts[1:]:
        factor_of = factor_of * one(*cut)
    return factor_of


def noise(rng, dims, deviation, reach, cuts=(), held_as=jnp.bfloat16):
    values = deviation * jax.random.normal(rng, dims, jnp.float32)
    if cuts:
        values = values * block_levels(rng, dims, cuts, -0.22, 0.18)
    return jnp.clip(values, -reach, reach).astype(held_as)


def setup_inputs(seed: int = 0) -> dict:
    key_list = jax.random.split(jax.random.key(seed), 6)
    return {
        "coarse_vectors": draw_coarse_vectors(jax.random.fold_in(key_list[5], 71), 0),
        "self_links": draw_self_links(jax.random.fold_in(key_list[5], 71), 0),
        "hop_links": draw_hop_links(jax.random.fold_in(key_list[5], 71), 0),
        "basis": noise(key_list[3], (NZB, NTB, BX, BY, 2 * BASIS, FINE), (2 * BASIS) ** -0.5, 0.5, ((0, 16), (1, 48))),
        "selected": draw_selected(jax.random.fold_in(key_list[5], 71), 0),
    }


HIGHEST = lax.Precision.HIGHEST

def block_product(vectors, links):
    return jnp.einsum('ztxyni,ztxyij->ztxynj', vectors, links, precision=HIGHEST)

def block_transposed(vectors, links):
    return jnp.einsum('ztxyni,ztxyji->ztxynj', vectors, links, precision=HIGHEST)

def apply_operator(vectors, self_full, hop_full):
    output = block_product(vectors, self_full)
    for hop_index, roll_axis in ((0, 2), (1, 3), (2, 0), (3, 1)):
        links_here = hop_full[hop_index]
        output = output + block_product(jnp.roll(vectors, -1, roll_axis), links_here)
        output = output + jnp.roll(block_transposed(vectors, links_here), 1, roll_axis)
    return output

def one_slab(carried):
    stacked, basis_slab = carried
    product = jnp.einsum('txyski,txyif->txyskf', stacked.astype(jnp.float32), basis_slab.astype(jnp.float32), precision=HIGHEST)
    return product.astype(jnp.bfloat16)

def reference(coarse_vectors, self_links, hop_links, basis, selected):
    self_full = self_links.astype(jnp.float32)
    hop_full = hop_links.astype(jnp.float32)

    def chebyshev_step(iteration, carried):
        earlier, current = carried
        return (current, 2.0 * apply_operator(current, self_full, hop_full) - earlier)
    first_image = apply_operator(coarse_vectors, self_full, hop_full)
    filtered = lax.fori_loop(0, DEG - 1, chebyshev_step, (coarse_vectors, first_image))[1]
    gram = jnp.einsum('ztxyni,ztxymi->nm', filtered, filtered, precision=HIGHEST)
    factor = jnp.linalg.cholesky(gram)
    onehot = (jnp.arange(NVEC, dtype=jnp.int32)[:, None] == selected[None, :]).astype(jnp.float32)
    total = NZB * NTB * BX * BY * 2 * BASIS
    rotation = lax.linalg.triangular_solve(factor, onehot, left_side=True, lower=True, transpose_a=True)
    rotation = rotation * jnp.sqrt(jnp.float32(total))
    coefficients = jnp.einsum('nk,ztxyni->ztxyki', rotation, filtered, precision=HIGHEST).astype(jnp.bfloat16)
    real_part = coefficients[..., :BASIS]
    imag_part = coefficients[..., BASIS:]
    stacked = jnp.stack([jnp.concatenate([real_part, -imag_part], -1), jnp.concatenate([imag_part, real_part], -1)], axis=4)
    return lax.map(one_slab, (stacked, basis))
```

```python
import functools

import jax
import jax.numpy as jnp
from jax import lax
from jax.experimental import pallas as pl
from jax.experimental.pallas import tpu as pltpu
from jax.sharding import Mesh, PartitionSpec as P

DEG = 16
HIGHEST = lax.Precision.HIGHEST
GZ = ("y", "c")
TA = ("x", "z")
TILE = 8


def shifted(value, axis, steps):
    count = lax.axis_size(axis)
    pairs = [(source, (source + steps) % count) for source in range(count)]
    return lax.ppermute(value, axis, pairs)


def exchanged(value, axis):
    return lax.all_to_all(value, axis, 0, 0, tiled=True)


def gathered(value, axis):
    count = lax.axis_size(axis)
    sent = jnp.broadcast_to(value[None], (count,) + value.shape)
    return exchanged(sent, axis)


def dot(left, right):
    return jnp.dot(left, right, precision=HIGHEST, preferred_element_type=jnp.float32)


def dot_t(left, right):
    return lax.dot_general(
        left,
        right,
        (((1,), (1,)), ((), ())),
        precision=HIGHEST,
        preferred_element_type=jnp.float32,
    )


def lower_inverse(matrix):
    size = matrix.shape[0]
    lane = lax.broadcasted_iota(jnp.int32, (TILE, size), 1)
    sublane = lax.broadcasted_iota(jnp.int32, (TILE, size), 0)
    groups = [matrix[g * TILE : (g + 1) * TILE, :] for g in range(size // TILE)]
    full = (TILE, size)
    for pivot in range(size):
        own, inner = divmod(pivot, TILE)
        row = jnp.broadcast_to(groups[own][inner : inner + 1, :], full)
        columns = {
            g: jnp.broadcast_to(groups[g][:, pivot : pivot + 1], full)
            for g in range(own, len(groups))
        }
        scale = 1.0 / jnp.broadcast_to(columns[own][inner : inner + 1, :], full)
        here = lane == pivot
        for g in range(own, len(groups)):
            factors = columns[g] * scale
            updated = jnp.where(here, -factors, groups[g] - factors * row)
            if g == own:
                updated = jnp.where(sublane > inner, updated, groups[g])
            groups[g] = updated
    result = []
    for g in range(len(groups)):
        rows = sublane + g * TILE
        diagonal = jnp.sum(jnp.where(lane == rows, groups[g], 0.0), axis=1, keepdims=True)
        unit = jnp.where(lane < rows, groups[g], jnp.where(lane == rows, 1.0, 0.0))
        result.append(unit * lax.rsqrt(diagonal))
    return jnp.concatenate(result, axis=0)


def select_kernel(scale, selected_ref, gram_ref, filtered_ref, out_ref, ortho_ref, coeff_ref):
    half = gram_ref.shape[1]
    first = lower_inverse(gram_ref[0:half, :])
    below = dot_t(gram_ref[half : 2 * half, :], first)
    second = lower_inverse(gram_ref[2 * half : 3 * half, :] - dot_t(below, below))
    top = dot(first, filtered_ref[0:half, :])
    ortho_ref[0:half, :] = top
    ortho_ref[half : 2 * half, :] = dot(second, filtered_ref[half : 2 * half, :] - dot(below, top))
    count = coeff_ref.shape[0]
    for k in range(count):
        coeff_ref[k : k + 1, :] = ortho_ref[pl.ds(selected_ref[k], 1), :]
    coefficients = (coeff_ref[...] * scale).astype(jnp.bfloat16).astype(jnp.float32)
    width = coefficients.shape[1]
    lane = lax.broadcasted_iota(jnp.int32, coefficients.shape, 1)
    out_ref[0:count, :] = jnp.where(lane < width // 2, coefficients, -coefficients).astype(
        jnp.bfloat16
    )
    swapped = jnp.concatenate(
        [coefficients[:, width // 2 :], coefficients[:, : width // 2]], axis=1
    )
    out_ref[count : 2 * count, :] = swapped.astype(jnp.bfloat16)


def gram_sum(gram):
    half = gram.shape[0] // 2
    packed = jnp.concatenate([gram[:half, :half], gram[half:, :half], gram[half:, half:]], axis=0)
    depth = lax.axis_size(GZ)
    share = exchanged(packed.reshape(depth, packed.shape[0] // depth, half), GZ).sum(axis=0)
    share = gathered(share, "x").sum(axis=0)
    share = gathered(share, "z").sum(axis=0)
    return gathered(share, GZ).reshape(packed.shape)


def local(coarse_vectors, self_links, hop_links, basis, selected):
    start = coarse_vectors[0, 0, 0, 0]
    hops = hop_links[:, 0, 0, 0, 0]
    below_z = shifted(hops[2], GZ, 1)
    below_t = shifted(hops[3], TA, 1)
    hop_x = hops[0].astype(jnp.float32)
    hop_y = hops[1].astype(jnp.float32)
    site = self_links[0, 0, 0, 0].astype(jnp.float32) + (hop_x + hop_x.T) + (hop_y + hop_y.T)
    around = jnp.concatenate([hops[2], below_z.T, hops[3], below_t.T], axis=0)

    def from_neighbours(vectors, links):
        sent = vectors.astype(jnp.bfloat16)
        halo = jnp.concatenate(
            [
                shifted(sent, GZ, -1),
                shifted(sent, GZ, 1),
                shifted(sent, TA, -1),
                shifted(sent, TA, 1),
            ],
            axis=1,
        )
        return jnp.dot(halo, links, preferred_element_type=jnp.float32)

    earlier = start
    current = dot(start, site) + from_neighbours(start, around)
    site2 = 2.0 * site
    around2 = 2.0 * around
    for _ in range(DEG - 1):
        near = dot(current, site2) - earlier
        earlier, current = current, near + from_neighbours(current, around2)
    filtered = current

    gram = gram_sum(dot_t(filtered, filtered))
    total = lax.axis_size(GZ) * lax.axis_size(TA) * start.shape[1]
    count = selected.shape[0]
    width = start.shape[1]
    stacked = pl.pallas_call(
        functools.partial(select_kernel, float(total) ** 0.5),
        out_shape=jax.ShapeDtypeStruct((2 * count, width), jnp.bfloat16),
        in_specs=[
            pl.BlockSpec(memory_space=pltpu.SMEM),
            pl.BlockSpec(memory_space=pltpu.VMEM),
            pl.BlockSpec(memory_space=pltpu.VMEM),
        ],
        out_specs=pl.BlockSpec(memory_space=pltpu.VMEM),
        scratch_shapes=[
            pltpu.VMEM(start.shape, jnp.float32),
            pltpu.VMEM((count, width), jnp.float32),
        ],
        compiler_params=pltpu.CompilerParams(vmem_limit_bytes=16 * 2**20),
    )(selected, gram, filtered)
    rebuilt = jnp.dot(stacked, basis[0, 0, 0, 0], preferred_element_type=jnp.float32)
    return rebuilt.astype(jnp.bfloat16).reshape(1, 1, 1, 1, 2, count, basis.shape[-1])


def solution(mesh):
    fine = Mesh(mesh.devices.reshape(8, 2, 4, 12), ("y", "c", "x", "z"))
    in_specs = (
        P(GZ, TA, None, None, None, None),
        P(GZ, TA, None, None, None, None),
        P(None, GZ, TA, None, None, None, None),
        P(GZ, TA, None, None, None, None),
        P(),
    )
    out_specs = P(GZ, TA, None, None, None, None, None)
    return jax.shard_map(local, mesh=fine, in_specs=in_specs, out_specs=out_specs, check_vma=False)
```

```python
import functools

import jax
import jax.numpy as jnp
from jax import lax
from jax.experimental import pallas as pl
from jax.experimental.pallas import tpu as pltpu
from jax.sharding import Mesh, PartitionSpec as P

DEG = 16
HIGHEST = lax.Precision.HIGHEST
GZ = ("y", "c")
TA = ("x", "z")
TILE = 8
REFINE_STEPS = 6
REFINE_ERROR = 1e-5


def shifted(value, axis, steps):
    count = lax.axis_size(axis)
    pairs = [(source, (source + steps) % count) for source in range(count)]
    return lax.ppermute(value, axis, pairs)


def exchanged(value, axis):
    return lax.all_to_all(value, axis, 0, 0, tiled=True)


def gathered(value, axis):
    count = lax.axis_size(axis)
    sent = jnp.broadcast_to(value[None], (count,) + value.shape)
    return exchanged(sent, axis)


def dot(left, right):
    return jnp.dot(left, right, precision=HIGHEST, preferred_element_type=jnp.float32)


def dot_t(left, right):
    return lax.dot_general(
        left,
        right,
        (((1,), (1,)), ((), ())),
        precision=HIGHEST,
        preferred_element_type=jnp.float32,
    )


def lower_inverse(matrix):
    size = matrix.shape[0]
    lane = lax.broadcasted_iota(jnp.int32, (TILE, size), 1)
    sublane = lax.broadcasted_iota(jnp.int32, (TILE, size), 0)
    groups = [matrix[g * TILE : (g + 1) * TILE, :] for g in range(size // TILE)]
    full = (TILE, size)
    for pivot in range(size):
        own, inner = divmod(pivot, TILE)
        row = jnp.broadcast_to(groups[own][inner : inner + 1, :], full)
        columns = {
            g: jnp.broadcast_to(groups[g][:, pivot : pivot + 1], full)
            for g in range(own, len(groups))
        }
        scale = 1.0 / jnp.broadcast_to(columns[own][inner : inner + 1, :], full)
        here = lane == pivot
        for g in range(own, len(groups)):
            factors = columns[g] * scale
            updated = jnp.where(here, -factors, groups[g] - factors * row)
            if g == own:
                updated = jnp.where(sublane > inner, updated, groups[g])
            groups[g] = updated
    result = []
    for g in range(len(groups)):
        rows = sublane + g * TILE
        diagonal = jnp.sum(jnp.where(lane == rows, groups[g], 0.0), axis=1, keepdims=True)
        unit = jnp.where(lane < rows, groups[g], jnp.where(lane == rows, 1.0, 0.0))
        result.append(unit * lax.rsqrt(diagonal))
    return jnp.concatenate(result, axis=0)


def split(value):
    high = value.astype(jnp.bfloat16)
    return high, (value - high.astype(jnp.float32)).astype(jnp.bfloat16)


def dot3(left, right, contract):
    dims = (((1,), (contract,)), ((), ()))
    (lh, ll), (rh, rl) = left, right
    one = functools.partial(
        lax.dot_general, dimension_numbers=dims, preferred_element_type=jnp.float32
    )
    return one(lh, rh) + (one(lh, rl) + one(ll, rh))


def select_kernel(scale, selected_ref, gram_ref, filtered_ref, out_ref, root_ref, picked_ref):
    size = root_ref.shape[0]
    half = size // 2
    first_block = gram_ref[0:half, :]
    cross_block = gram_ref[half : 2 * half, :]
    second_block = gram_ref[2 * half : 3 * half, :]
    gram = jnp.concatenate(
        [
            jnp.concatenate([first_block, cross_block.T], axis=1),
            jnp.concatenate([cross_block, second_block], axis=1),
        ],
        axis=0,
    )
    row = lax.broadcasted_iota(jnp.int32, gram.shape, 0)
    column = lax.broadcasted_iota(jnp.int32, gram.shape, 1)
    diagonal = jnp.where(row == column, gram, 0.0)
    across = lax.rsqrt(jnp.sum(diagonal, axis=0, keepdims=True))
    down = lax.rsqrt(jnp.sum(diagonal, axis=1, keepdims=True))
    scaled = gram * down * across
    scaled_parts = split(scaled)
    identity = jnp.where(row == column, 1.0, 0.0)
    root_ref[...] = jnp.where(row > column, -scaled, identity)

    def refine(state):
        step, _ = state
        root = split(root_ref[...])
        half_way = split(dot3(root, scaled_parts, 0))
        residual = dot3(half_way, root, 1) - identity
        lower = jnp.where(row > column, residual, 0.5 * identity * residual)
        root_ref[...] = root_ref[...] - dot3(split(lower), root, 0)
        return step + 1, jnp.sum(residual * residual)

    def unfinished(state):
        step, error = state
        return jnp.logical_and(step < REFINE_STEPS, error >= REFINE_ERROR)

    _, error = lax.while_loop(unfinished, refine, (jnp.int32(0), jnp.float32(1.0)))
    refined = error < REFINE_ERROR

    @pl.when(refined)
    def _():
        root_ref[...] = root_ref[...] * across

    @pl.when(jnp.logical_not(refined))
    def _():
        first = lower_inverse(gram_ref[0:half, :])
        below = dot_t(gram_ref[half : 2 * half, :], first)
        second = lower_inverse(gram_ref[2 * half : 3 * half, :] - dot_t(below, below))
        root_ref[0:half, 0:half] = first
        root_ref[0:half, half:size] = jnp.zeros((half, half), jnp.float32)
        root_ref[half:size, 0:half] = -dot(second, dot(below, first))
        root_ref[half:size, half:size] = second

    count = picked_ref.shape[0]
    for k in range(count):
        picked_ref[k : k + 1, :] = root_ref[pl.ds(selected_ref[k], 1), :]
    coefficients = dot(picked_ref[...] * scale, filtered_ref[...])
    coefficients = coefficients.astype(jnp.bfloat16).astype(jnp.float32)
    width = coefficients.shape[1]
    lane = lax.broadcasted_iota(jnp.int32, coefficients.shape, 1)
    out_ref[0:count, :] = jnp.where(lane < width // 2, coefficients, -coefficients).astype(
        jnp.bfloat16
    )
    swapped = jnp.concatenate(
        [coefficients[:, width // 2 :], coefficients[:, : width // 2]], axis=1
    )
    out_ref[count : 2 * count, :] = swapped.astype(jnp.bfloat16)


def rebuild_rows(selected, gram, filtered, scale):
    count = selected.shape[0]
    size, width = filtered.shape
    vmem = pl.BlockSpec(memory_space=pltpu.VMEM)
    return pl.pallas_call(
        functools.partial(select_kernel, scale),
        out_shape=jax.ShapeDtypeStruct((2 * count, width), jnp.bfloat16),
        in_specs=[pl.BlockSpec(memory_space=pltpu.SMEM), vmem, vmem],
        out_specs=vmem,
        scratch_shapes=[
            pltpu.VMEM((size, size), jnp.float32),
            pltpu.VMEM((count, size), jnp.float32),
        ],
        compiler_params=pltpu.CompilerParams(vmem_limit_bytes=16 * 2**20),
    )(selected, gram, filtered)


def gram_sum(gram):
    half = gram.shape[0] // 2
    packed = jnp.concatenate([gram[:half, :half], gram[half:, :half], gram[half:, half:]], axis=0)
    around = ("y", "x")
    depth = lax.axis_size(around)
    share = exchanged(packed.reshape(depth, packed.shape[0] // depth, half), around).sum(axis=0)
    share = share + shifted(share, "c", 1)
    share = gathered(share, "z").sum(axis=0)
    return gathered(share, around).reshape(packed.shape)


def local(coarse_vectors, self_links, hop_links, basis, selected):
    start = coarse_vectors[0, 0, 0, 0]
    hops = hop_links[:, 0, 0, 0, 0]
    below_z = shifted(hops[2], GZ, 1)
    below_t = shifted(hops[3], TA, 1)
    hop_x = hops[0].astype(jnp.float32)
    hop_y = hops[1].astype(jnp.float32)
    site = self_links[0, 0, 0, 0].astype(jnp.float32) + (hop_x + hop_x.T) + (hop_y + hop_y.T)
    around = jnp.concatenate([hops[2], below_z.T, hops[3], below_t.T], axis=0)

    def from_neighbours(vectors, links):
        sent = vectors.astype(jnp.bfloat16)
        halo = jnp.concatenate(
            [
                shifted(sent, GZ, -1),
                shifted(sent, GZ, 1),
                shifted(sent, TA, -1),
                shifted(sent, TA, 1),
            ],
            axis=1,
        )
        return jnp.dot(halo, links, preferred_element_type=jnp.float32)

    earlier = start
    current = dot(start, site) + from_neighbours(start, around)
    site2 = 2.0 * site
    around2 = 2.0 * around
    for _ in range(DEG - 1):
        near = dot(current, site2) - earlier
        earlier, current = current, near + from_neighbours(current, around2)
    filtered = current

    gram = gram_sum(dot_t(filtered, filtered))
    total = lax.axis_size(GZ) * lax.axis_size(TA) * start.shape[1]
    count = selected.shape[0]
    stacked = rebuild_rows(selected, gram, filtered, float(total) ** 0.5)
    rebuilt = jnp.dot(stacked, basis[0, 0, 0, 0], preferred_element_type=jnp.float32)
    return rebuilt.astype(jnp.bfloat16).reshape(1, 1, 1, 1, 2, count, basis.shape[-1])


def solution(mesh):
    fine = Mesh(mesh.devices.reshape(8, 2, 4, 12), ("y", "c", "x", "z"))
    in_specs = (
        P(GZ, TA, None, None, None, None),
        P(GZ, TA, None, None, None, None),
        P(None, GZ, TA, None, None, None, None),
        P(GZ, TA, None, None, None, None),
        P(),
    )
    out_specs = P(GZ, TA, None, None, None, None, None)
    return jax.shard_map(local, mesh=fine, in_specs=in_specs, out_specs=out_specs, check_vma=False)
```

```python
import functools

import jax
import jax.numpy as jnp
from jax import lax
from jax.experimental import pallas as pl
from jax.experimental.pallas import tpu as pltpu
from jax.sharding import Mesh, PartitionSpec as P

DEG = 16
HIGHEST = lax.Precision.HIGHEST
GZ = ("y", "c")
TA = ("x", "z")
TILE = 8
REFINE_STEPS = 6
REFINE_ERROR = 1e-5


def shifted(value, axis, steps):
    count = lax.axis_size(axis)
    pairs = [(source, (source + steps) % count) for source in range(count)]
    return lax.ppermute(value, axis, pairs)


def along(site):
    rows, places = lax.axis_size("x"), lax.axis_size("z")
    row, place = divmod(site % (rows * places), places)
    return row * places + (place if row % 2 == 0 else places - 1 - place)


def reordered(value, steps=0):
    pairs = [(site, along(site + steps)) for site in range(lax.axis_size(TA))]
    return lax.ppermute(value, TA, pairs)


def reordered_above(value):
    depth, count = lax.axis_size(GZ), lax.axis_size(TA)
    pairs = [
        (layer * count + site, (layer + 1) % depth * count + along(site))
        for layer in range(depth)
        for site in range(count)
    ]
    return lax.ppermute(value, GZ + TA, pairs)


def shifted_along(value, steps):
    pairs = [(along(site), along(site + steps)) for site in range(lax.axis_size(TA))]
    return lax.ppermute(value, TA, pairs)


def exchanged(value, axis):
    return lax.all_to_all(value, axis, 0, 0, tiled=True)


def gathered(value, axis):
    count = lax.axis_size(axis)
    sent = jnp.broadcast_to(value[None], (count,) + value.shape)
    return exchanged(sent, axis)


def dot(left, right):
    return jnp.dot(left, right, precision=HIGHEST, preferred_element_type=jnp.float32)


def dot_t(left, right):
    return lax.dot_general(
        left,
        right,
        (((1,), (1,)), ((), ())),
        precision=HIGHEST,
        preferred_element_type=jnp.float32,
    )


def lower_inverse(matrix):
    size = matrix.shape[0]
    lane = lax.broadcasted_iota(jnp.int32, (TILE, size), 1)
    sublane = lax.broadcasted_iota(jnp.int32, (TILE, size), 0)
    groups = [matrix[g * TILE : (g + 1) * TILE, :] for g in range(size // TILE)]
    full = (TILE, size)
    for pivot in range(size):
        own, inner = divmod(pivot, TILE)
        row = jnp.broadcast_to(groups[own][inner : inner + 1, :], full)
        columns = {
            g: jnp.broadcast_to(groups[g][:, pivot : pivot + 1], full)
            for g in range(own, len(groups))
        }
        scale = 1.0 / jnp.broadcast_to(columns[own][inner : inner + 1, :], full)
        here = lane == pivot
        for g in range(own, len(groups)):
            factors = columns[g] * scale
            updated = jnp.where(here, -factors, groups[g] - factors * row)
            if g == own:
                updated = jnp.where(sublane > inner, updated, groups[g])
            groups[g] = updated
    result = []
    for g in range(len(groups)):
        rows = sublane + g * TILE
        diagonal = jnp.sum(jnp.where(lane == rows, groups[g], 0.0), axis=1, keepdims=True)
        unit = jnp.where(lane < rows, groups[g], jnp.where(lane == rows, 1.0, 0.0))
        result.append(unit * lax.rsqrt(diagonal))
    return jnp.concatenate(result, axis=0)


def split(value):
    high = value.astype(jnp.bfloat16)
    return high, (value - high.astype(jnp.float32)).astype(jnp.bfloat16)


def dot3(left, right, contract):
    dims = (((1,), (contract,)), ((), ()))
    (lh, ll), (rh, rl) = left, right
    one = functools.partial(
        lax.dot_general, dimension_numbers=dims, preferred_element_type=jnp.float32
    )
    return one(lh, rh) + (one(lh, rl) + one(ll, rh))


def select_kernel(scale, selected_ref, gram_ref, filtered_ref, out_ref, root_ref, picked_ref):
    size = root_ref.shape[0]
    half = size // 2
    first_block = gram_ref[0:half, :]
    cross_block = gram_ref[half : 2 * half, :]
    second_block = gram_ref[2 * half : 3 * half, :]
    gram = jnp.concatenate(
        [
            jnp.concatenate([first_block, cross_block.T], axis=1),
            jnp.concatenate([cross_block, second_block], axis=1),
        ],
        axis=0,
    )
    row = lax.broadcasted_iota(jnp.int32, gram.shape, 0)
    column = lax.broadcasted_iota(jnp.int32, gram.shape, 1)
    diagonal = jnp.where(row == column, gram, 0.0)
    across = lax.rsqrt(jnp.sum(diagonal, axis=0, keepdims=True))
    down = lax.rsqrt(jnp.sum(diagonal, axis=1, keepdims=True))
    scaled = gram * down * across
    scaled_parts = split(scaled)
    identity = jnp.where(row == column, 1.0, 0.0)
    root_ref[...] = jnp.where(row > column, -scaled, identity)

    def refine(state):
        step, _ = state
        root = split(root_ref[...])
        half_way = split(dot3(root, scaled_parts, 0))
        residual = dot3(half_way, root, 1) - identity
        lower = jnp.where(row > column, residual, 0.5 * identity * residual)
        root_ref[...] = root_ref[...] - dot3(split(lower), root, 0)
        return step + 1, jnp.sum(residual * residual)

    def unfinished(state):
        step, error = state
        return jnp.logical_and(step < REFINE_STEPS, error >= REFINE_ERROR)

    _, error = lax.while_loop(unfinished, refine, (jnp.int32(0), jnp.float32(1.0)))
    refined = error < REFINE_ERROR

    @pl.when(refined)
    def _():
        root_ref[...] = root_ref[...] * across

    @pl.when(jnp.logical_not(refined))
    def _():
        first = lower_inverse(gram_ref[0:half, :])
        below = dot_t(gram_ref[half : 2 * half, :], first)
        second = lower_inverse(gram_ref[2 * half : 3 * half, :] - dot_t(below, below))
        root_ref[0:half, 0:half] = first
        root_ref[0:half, half:size] = jnp.zeros((half, half), jnp.float32)
        root_ref[half:size, 0:half] = -dot(second, dot(below, first))
        root_ref[half:size, half:size] = second

    count = picked_ref.shape[0]
    for k in range(count):
        picked_ref[k : k + 1, :] = root_ref[pl.ds(selected_ref[k], 1), :]
    coefficients = dot(picked_ref[...] * scale, filtered_ref[...])
    coefficients = coefficients.astype(jnp.bfloat16).astype(jnp.float32)
    width = coefficients.shape[1]
    lane = lax.broadcasted_iota(jnp.int32, coefficients.shape, 1)
    out_ref[0:count, :] = jnp.where(lane < width // 2, coefficients, -coefficients).astype(
        jnp.bfloat16
    )
    swapped = jnp.concatenate(
        [coefficients[:, width // 2 :], coefficients[:, : width // 2]], axis=1
    )
    out_ref[count : 2 * count, :] = swapped.astype(jnp.bfloat16)


def rebuild_rows(selected, gram, filtered, scale):
    count = selected.shape[0]
    size, width = filtered.shape
    vmem = pl.BlockSpec(memory_space=pltpu.VMEM)
    return pl.pallas_call(
        functools.partial(select_kernel, scale),
        out_shape=jax.ShapeDtypeStruct((2 * count, width), jnp.bfloat16),
        in_specs=[pl.BlockSpec(memory_space=pltpu.SMEM), vmem, vmem],
        out_specs=vmem,
        scratch_shapes=[
            pltpu.VMEM((size, size), jnp.float32),
            pltpu.VMEM((count, size), jnp.float32),
        ],
        compiler_params=pltpu.CompilerParams(vmem_limit_bytes=16 * 2**20),
    )(selected, gram, filtered)


def gram_sum(gram):
    half = gram.shape[0] // 2
    packed = jnp.concatenate([gram[:half, :half], gram[half:, :half], gram[half:, half:]], axis=0)
    around = ("y", "x")
    depth = lax.axis_size(around)
    share = exchanged(packed.reshape(depth, packed.shape[0] // depth, half), around).sum(axis=0)
    share = share + shifted(share, "c", 1)
    share = gathered(share, "z").sum(axis=0)
    return gathered(share, around).reshape(packed.shape)


def local(coarse_vectors, self_links, hop_links, basis, selected):
    start = reordered(coarse_vectors[0, 0, 0, 0])
    hops = hop_links[:, 0, 0, 0, 0]
    hop_x = hops[0].astype(jnp.float32)
    hop_y = hops[1].astype(jnp.float32)
    site = self_links[0, 0, 0, 0].astype(jnp.float32) + (hop_x + hop_x.T) + (hop_y + hop_y.T)
    width = site.shape[0]
    own = reordered(jnp.concatenate([*split(site), hops[2], hops[3]], axis=0))
    site = own[:width].astype(jnp.float32) + own[width : 2 * width].astype(jnp.float32)
    above_z, above_t = own[2 * width : 3 * width], own[3 * width :]
    below_z = reordered_above(hops[2].T)
    below_t = reordered(hops[3].T, 1)
    around = jnp.concatenate([above_t, below_t, above_z, below_z], axis=0)

    def from_neighbours(vectors, links):
        sent = vectors.astype(jnp.bfloat16)
        halo = jnp.concatenate(
            [
                shifted_along(sent, -1),
                shifted_along(sent, 1),
                shifted(sent, GZ, -1),
                shifted(sent, GZ, 1),
            ],
            axis=1,
        )
        return jnp.dot(halo, links, preferred_element_type=jnp.float32)

    earlier = start
    current = dot(start, site) + from_neighbours(start, around)
    site2 = 2.0 * site
    around2 = 2.0 * around
    for _ in range(DEG - 1):
        near = dot(current, site2) - earlier
        earlier, current = current, near + from_neighbours(current, around2)
    filtered = reordered(current)

    gram = gram_sum(dot_t(current, current))
    total = lax.axis_size(GZ) * lax.axis_size(TA) * start.shape[1]
    count = selected.shape[0]
    stacked = rebuild_rows(selected, gram, filtered, float(total) ** 0.5)
    rebuilt = jnp.dot(stacked, basis[0, 0, 0, 0], preferred_element_type=jnp.float32)
    return rebuilt.astype(jnp.bfloat16).reshape(1, 1, 1, 1, 2, count, basis.shape[-1])


def solution(mesh):
    fine = Mesh(mesh.devices.reshape(8, 2, 4, 12), ("y", "c", "x", "z"))
    in_specs = (
        P(GZ, TA, None, None, None, None),
        P(GZ, TA, None, None, None, None),
        P(None, GZ, TA, None, None, None, None),
        P(GZ, TA, None, None, None, None),
        P(),
    )
    out_specs = P(GZ, TA, None, None, None, None, None)
    return jax.shard_map(local, mesh=fine, in_specs=in_specs, out_specs=out_specs, check_vma=False)
```

```python
import functools

import jax
import jax.numpy as jnp
from jax import lax
from jax.experimental import pallas as pl
from jax.experimental.pallas import tpu as pltpu
from jax.sharding import Mesh, PartitionSpec as P

DEG = 16
HIGHEST = lax.Precision.HIGHEST
GZ = ("y", "c")
TA = ("x", "z")
TILE = 8
REFINE_STEPS = 6
REFINE_ERROR = 1e-5


def shifted(value, axis, steps):
    count = lax.axis_size(axis)
    pairs = [(source, (source + steps) % count) for source in range(count)]
    return lax.ppermute(value, axis, pairs)


def along(site):
    rows, places = lax.axis_size("x"), lax.axis_size("z")
    row, place = divmod(site % (rows * places), places)
    return row * places + (place if row % 2 == 0 else places - 1 - place)


def reordered(value):
    pairs = [(site, along(site)) for site in range(lax.axis_size(TA))]
    return lax.ppermute(value, TA, pairs)


def shifted_along(value, steps):
    pairs = [(along(site), along(site + steps)) for site in range(lax.axis_size(TA))]
    return lax.ppermute(value, TA, pairs)


def exchanged(value, axis):
    return lax.all_to_all(value, axis, 0, 0, tiled=True)


def gathered(value, axis):
    count = lax.axis_size(axis)
    sent = jnp.broadcast_to(value[None], (count,) + value.shape)
    return exchanged(sent, axis)


def dot(left, right):
    return jnp.dot(left, right, precision=HIGHEST, preferred_element_type=jnp.float32)


def dot_t(left, right):
    return lax.dot_general(
        left,
        right,
        (((1,), (1,)), ((), ())),
        precision=HIGHEST,
        preferred_element_type=jnp.float32,
    )


def lower_inverse(matrix):
    size = matrix.shape[0]
    lane = lax.broadcasted_iota(jnp.int32, (TILE, size), 1)
    sublane = lax.broadcasted_iota(jnp.int32, (TILE, size), 0)
    groups = [matrix[g * TILE : (g + 1) * TILE, :] for g in range(size // TILE)]
    full = (TILE, size)
    for pivot in range(size):
        own, inner = divmod(pivot, TILE)
        row = jnp.broadcast_to(groups[own][inner : inner + 1, :], full)
        columns = {
            g: jnp.broadcast_to(groups[g][:, pivot : pivot + 1], full)
            for g in range(own, len(groups))
        }
        scale = 1.0 / jnp.broadcast_to(columns[own][inner : inner + 1, :], full)
        here = lane == pivot
        for g in range(own, len(groups)):
            factors = columns[g] * scale
            updated = jnp.where(here, -factors, groups[g] - factors * row)
            if g == own:
                updated = jnp.where(sublane > inner, updated, groups[g])
            groups[g] = updated
    result = []
    for g in range(len(groups)):
        rows = sublane + g * TILE
        diagonal = jnp.sum(jnp.where(lane == rows, groups[g], 0.0), axis=1, keepdims=True)
        unit = jnp.where(lane < rows, groups[g], jnp.where(lane == rows, 1.0, 0.0))
        result.append(unit * lax.rsqrt(diagonal))
    return jnp.concatenate(result, axis=0)


def split(value):
    high = value.astype(jnp.bfloat16)
    return high, (value - high.astype(jnp.float32)).astype(jnp.bfloat16)


def dot3(left, right, contract):
    dims = (((1,), (contract,)), ((), ()))
    (lh, ll), (rh, rl) = left, right
    one = functools.partial(
        lax.dot_general, dimension_numbers=dims, preferred_element_type=jnp.float32
    )
    return one(lh, rh) + (one(lh, rl) + one(ll, rh))


def select_kernel(scale, selected_ref, gram_ref, filtered_ref, out_ref, root_ref, picked_ref):
    size = root_ref.shape[0]
    half = size // 2
    first_block = gram_ref[0:half, :]
    cross_block = gram_ref[half : 2 * half, :]
    second_block = gram_ref[2 * half : 3 * half, :]
    gram = jnp.concatenate(
        [
            jnp.concatenate([first_block, cross_block.T], axis=1),
            jnp.concatenate([cross_block, second_block], axis=1),
        ],
        axis=0,
    )
    row = lax.broadcasted_iota(jnp.int32, gram.shape, 0)
    column = lax.broadcasted_iota(jnp.int32, gram.shape, 1)
    diagonal = jnp.where(row == column, gram, 0.0)
    across = lax.rsqrt(jnp.sum(diagonal, axis=0, keepdims=True))
    down = lax.rsqrt(jnp.sum(diagonal, axis=1, keepdims=True))
    scaled = gram * down * across
    scaled_parts = split(scaled)
    identity = jnp.where(row == column, 1.0, 0.0)
    root_ref[...] = jnp.where(row > column, -scaled, identity)

    def refine(state):
        step, _ = state
        root = split(root_ref[...])
        half_way = split(dot3(root, scaled_parts, 0))
        residual = dot3(half_way, root, 1) - identity
        lower = jnp.where(row > column, residual, 0.5 * identity * residual)
        root_ref[...] = root_ref[...] - dot3(split(lower), root, 0)
        return step + 1, jnp.sum(residual * residual)

    def unfinished(state):
        step, error = state
        return jnp.logical_and(step < REFINE_STEPS, error >= REFINE_ERROR)

    _, error = lax.while_loop(unfinished, refine, (jnp.int32(0), jnp.float32(1.0)))
    refined = error < REFINE_ERROR

    @pl.when(refined)
    def _():
        root_ref[...] = root_ref[...] * across

    @pl.when(jnp.logical_not(refined))
    def _():
        first = lower_inverse(gram_ref[0:half, :])
        below = dot_t(gram_ref[half : 2 * half, :], first)
        second = lower_inverse(gram_ref[2 * half : 3 * half, :] - dot_t(below, below))
        root_ref[0:half, 0:half] = first
        root_ref[0:half, half:size] = jnp.zeros((half, half), jnp.float32)
        root_ref[half:size, 0:half] = -dot(second, dot(below, first))
        root_ref[half:size, half:size] = second

    count = picked_ref.shape[0]
    for k in range(count):
        picked_ref[k : k + 1, :] = root_ref[pl.ds(selected_ref[k], 1), :]
    coefficients = dot(picked_ref[...] * scale, filtered_ref[...])
    coefficients = coefficients.astype(jnp.bfloat16).astype(jnp.float32)
    width = coefficients.shape[1]
    lane = lax.broadcasted_iota(jnp.int32, coefficients.shape, 1)
    out_ref[0:count, :] = jnp.where(lane < width // 2, coefficients, -coefficients).astype(
        jnp.bfloat16
    )
    swapped = jnp.concatenate(
        [coefficients[:, width // 2 :], coefficients[:, : width // 2]], axis=1
    )
    out_ref[count : 2 * count, :] = swapped.astype(jnp.bfloat16)


def rebuild_rows(selected, gram, filtered, scale):
    count = selected.shape[0]
    size, width = filtered.shape
    vmem = pl.BlockSpec(memory_space=pltpu.VMEM)
    return pl.pallas_call(
        functools.partial(select_kernel, scale),
        out_shape=jax.ShapeDtypeStruct((2 * count, width), jnp.bfloat16),
        in_specs=[pl.BlockSpec(memory_space=pltpu.SMEM), vmem, vmem],
        out_specs=vmem,
        scratch_shapes=[
            pltpu.VMEM((size, size), jnp.float32),
            pltpu.VMEM((count, size), jnp.float32),
        ],
        compiler_params=pltpu.CompilerParams(vmem_limit_bytes=16 * 2**20),
    )(selected, gram, filtered)


def gram_sum(gram):
    half = gram.shape[0] // 2
    packed = jnp.concatenate([gram[:half, :half], gram[half:, :half], gram[half:, half:]], axis=0)
    around = ("y", "x")
    depth = lax.axis_size(around)
    share = exchanged(packed.reshape(depth, packed.shape[0] // depth, half), around).sum(axis=0)
    share = share + shifted(share, "c", 1)
    share = gathered(share, "z").sum(axis=0)
    return gathered(share, around).reshape(packed.shape)


def local(coarse_vectors, self_links, hop_links, basis, selected):
    start = reordered(coarse_vectors[0, 0, 0, 0])
    hops = hop_links[:, 0, 0, 0, 0]
    hop_x = hops[0].astype(jnp.float32)
    hop_y = hops[1].astype(jnp.float32)
    site = self_links[0, 0, 0, 0].astype(jnp.float32) + (hop_x + hop_x.T) + (hop_y + hop_y.T)
    width = site.shape[0]
    site_high = lax.reduce_precision(site, 8, 7)
    parts = [site_high.astype(jnp.bfloat16), (site - site_high).astype(jnp.bfloat16)]
    own = reordered(jnp.concatenate([*parts, hops[2], hops[3]], axis=0))
    site = own[:width].astype(jnp.float32) + own[width : 2 * width].astype(jnp.float32)
    above_z, above_t = own[2 * width : 3 * width], own[3 * width :]

    def halos(down_t, up_t, up_z, down_z):
        from_below_t = shifted_along(up_t, 1)
        from_above_t = shifted_along(down_t, -1)
        from_below_z = shifted(up_z, GZ, 1)
        from_above_z = shifted(down_z, GZ, -1)
        return from_below_t, from_above_t, from_below_z, from_above_z

    def product(halo, links):
        halo = jnp.concatenate(halo, axis=1)
        return jnp.dot(halo, links, preferred_element_type=jnp.float32)

    sent = start.astype(jnp.bfloat16)
    up_t = jnp.concatenate([sent, above_t.T], axis=0)
    up_z = jnp.concatenate([sent, above_z.T], axis=0)
    count = sent.shape[0]
    near_t, far_t, near_z, far_z = halos(sent, up_t, up_z, sent)
    around = jnp.concatenate([near_t[count:], above_t, near_z[count:], above_z], axis=0)
    halo = near_t[:count], far_t, near_z[:count], far_z

    earlier = start
    current = dot(start, site) + product(halo, around)
    site2 = 2.0 * site
    around2 = 2.0 * around
    for _ in range(DEG - 1):
        near = dot(current, site2) - earlier
        sent = current.astype(jnp.bfloat16)
        halo = halos(sent, sent, sent, sent)
        earlier, current = current, near + product(halo, around2)
    filtered = reordered(current)

    gram = gram_sum(dot_t(current, current))
    total = lax.axis_size(GZ) * lax.axis_size(TA) * start.shape[1]
    count = selected.shape[0]
    stacked = rebuild_rows(selected, gram, filtered, float(total) ** 0.5)
    rebuilt = jnp.dot(stacked, basis[0, 0, 0, 0], preferred_element_type=jnp.float32)
    return rebuilt.astype(jnp.bfloat16).reshape(1, 1, 1, 1, 2, count, basis.shape[-1])


def solution(mesh):
    fine = Mesh(mesh.devices.reshape(8, 2, 4, 12), ("y", "c", "x", "z"))
    in_specs = (
        P(GZ, TA, None, None, None, None),
        P(GZ, TA, None, None, None, None),
        P(None, GZ, TA, None, None, None, None),
        P(GZ, TA, None, None, None, None),
        P(),
    )
    out_specs = P(GZ, TA, None, None, None, None, None)
    return jax.shard_map(local, mesh=fine, in_specs=in_specs, out_specs=out_specs, check_vma=False)
```

```python
import functools

import jax
import jax.numpy as jnp
from jax import lax
from jax.experimental import pallas as pl
from jax.experimental.pallas import tpu as pltpu
from jax.sharding import Mesh, PartitionSpec as P

DEG = 16
HIGHEST = lax.Precision.HIGHEST
GZ = ("y", "c")
TA = ("x", "z")
TILE = 8
REFINE_STEPS = 6
REFINE_ERROR = 1e-5


def shifted(value, axis, steps):
    count = lax.axis_size(axis)
    pairs = [(source, (source + steps) % count) for source in range(count)]
    return lax.ppermute(value, axis, pairs)


def along(site):
    rows, places = lax.axis_size("x"), lax.axis_size("z")
    row, place = divmod(site % (rows * places), places)
    return row * places + (place if row % 2 == 0 else places - 1 - place)


def reordered(value):
    pairs = [(site, along(site)) for site in range(lax.axis_size(TA))]
    return lax.ppermute(value, TA, pairs)


def shifted_along(value, steps):
    pairs = [(along(site), along(site + steps)) for site in range(lax.axis_size(TA))]
    return lax.ppermute(value, TA, pairs)


def exchanged(value, axis):
    return lax.all_to_all(value, axis, 0, 0, tiled=True)


def gathered(value, axis):
    count = lax.axis_size(axis)
    sent = jnp.broadcast_to(value[None], (count,) + value.shape)
    return exchanged(sent, axis)


def dot(left, right):
    return jnp.dot(left, right, precision=HIGHEST, preferred_element_type=jnp.float32)


def dot_t(left, right):
    return lax.dot_general(
        left,
        right,
        (((1,), (1,)), ((), ())),
        precision=HIGHEST,
        preferred_element_type=jnp.float32,
    )


def lower_inverse(matrix):
    size = matrix.shape[0]
    lane = lax.broadcasted_iota(jnp.int32, (TILE, size), 1)
    sublane = lax.broadcasted_iota(jnp.int32, (TILE, size), 0)
    groups = [matrix[g * TILE : (g + 1) * TILE, :] for g in range(size // TILE)]
    full = (TILE, size)
    for pivot in range(size):
        own, inner = divmod(pivot, TILE)
        row = jnp.broadcast_to(groups[own][inner : inner + 1, :], full)
        columns = {
            g: jnp.broadcast_to(groups[g][:, pivot : pivot + 1], full)
            for g in range(own, len(groups))
        }
        scale = 1.0 / jnp.broadcast_to(columns[own][inner : inner + 1, :], full)
        here = lane == pivot
        for g in range(own, len(groups)):
            factors = columns[g] * scale
            updated = jnp.where(here, -factors, groups[g] - factors * row)
            if g == own:
                updated = jnp.where(sublane > inner, updated, groups[g])
            groups[g] = updated
    result = []
    for g in range(len(groups)):
        rows = sublane + g * TILE
        diagonal = jnp.sum(jnp.where(lane == rows, groups[g], 0.0), axis=1, keepdims=True)
        unit = jnp.where(lane < rows, groups[g], jnp.where(lane == rows, 1.0, 0.0))
        result.append(unit * lax.rsqrt(diagonal))
    return jnp.concatenate(result, axis=0)


def split(value):
    high = value.astype(jnp.bfloat16)
    return high, (value - high.astype(jnp.float32)).astype(jnp.bfloat16)


def dot3(left, right, contract):
    dims = (((1,), (contract,)), ((), ()))
    (lh, ll), (rh, rl) = left, right
    one = functools.partial(
        lax.dot_general, dimension_numbers=dims, preferred_element_type=jnp.float32
    )
    return one(lh, rh) + (one(lh, rl) + one(ll, rh))


def select_kernel(scale, selected_ref, gram_ref, filtered_ref, out_ref, root_ref, picked_ref):
    size = root_ref.shape[0]
    half = size // 2
    first_block = gram_ref[0:half, :]
    cross_block = gram_ref[half : 2 * half, :]
    second_block = gram_ref[2 * half : 3 * half, :]
    gram = jnp.concatenate(
        [
            jnp.concatenate([first_block, cross_block.T], axis=1),
            jnp.concatenate([cross_block, second_block], axis=1),
        ],
        axis=0,
    )
    row = lax.broadcasted_iota(jnp.int32, gram.shape, 0)
    column = lax.broadcasted_iota(jnp.int32, gram.shape, 1)
    diagonal = jnp.where(row == column, gram, 0.0)
    across = lax.rsqrt(jnp.sum(diagonal, axis=0, keepdims=True))
    down = lax.rsqrt(jnp.sum(diagonal, axis=1, keepdims=True))
    scaled = gram * down * across
    scaled_parts = split(scaled)
    identity = jnp.where(row == column, 1.0, 0.0)
    root_ref[...] = jnp.where(row > column, -scaled, identity)

    def refine(state):
        step, _ = state
        root = split(root_ref[...])
        half_way = split(dot3(root, scaled_parts, 0))
        residual = dot3(half_way, root, 1) - identity
        lower = jnp.where(row > column, residual, 0.5 * identity * residual)
        root_ref[...] = root_ref[...] - dot3(split(lower), root, 0)
        return step + 1, jnp.sum(residual * residual)

    def unfinished(state):
        step, error = state
        return jnp.logical_and(step < REFINE_STEPS, error >= REFINE_ERROR)

    _, error = lax.while_loop(unfinished, refine, (jnp.int32(0), jnp.float32(1.0)))
    refined = error < REFINE_ERROR

    @pl.when(refined)
    def _():
        root_ref[...] = root_ref[...] * across

    @pl.when(jnp.logical_not(refined))
    def _():
        first = lower_inverse(gram_ref[0:half, :])
        below = dot_t(gram_ref[half : 2 * half, :], first)
        second = lower_inverse(gram_ref[2 * half : 3 * half, :] - dot_t(below, below))
        root_ref[0:half, 0:half] = first
        root_ref[0:half, half:size] = jnp.zeros((half, half), jnp.float32)
        root_ref[half:size, 0:half] = -dot(second, dot(below, first))
        root_ref[half:size, half:size] = second

    count = picked_ref.shape[0]
    for k in range(count):
        picked_ref[k : k + 1, :] = root_ref[pl.ds(selected_ref[k], 1), :]
    coefficients = dot(picked_ref[...] * scale, filtered_ref[...])
    coefficients = coefficients.astype(jnp.bfloat16).astype(jnp.float32)
    width = coefficients.shape[1]
    lane = lax.broadcasted_iota(jnp.int32, coefficients.shape, 1)
    out_ref[0:count, :] = jnp.where(lane < width // 2, coefficients, -coefficients).astype(
        jnp.bfloat16
    )
    swapped = jnp.concatenate(
        [coefficients[:, width // 2 :], coefficients[:, : width // 2]], axis=1
    )
    out_ref[count : 2 * count, :] = swapped.astype(jnp.bfloat16)


def rebuild_rows(selected, gram, filtered, scale):
    count = selected.shape[0]
    size, width = filtered.shape
    vmem = pl.BlockSpec(memory_space=pltpu.VMEM)
    return pl.pallas_call(
        functools.partial(select_kernel, scale),
        out_shape=jax.ShapeDtypeStruct((2 * count, width), jnp.bfloat16),
        in_specs=[pl.BlockSpec(memory_space=pltpu.SMEM), vmem, vmem],
        out_specs=vmem,
        scratch_shapes=[
            pltpu.VMEM((size, size), jnp.float32),
            pltpu.VMEM((count, size), jnp.float32),
        ],
        compiler_params=pltpu.CompilerParams(vmem_limit_bytes=16 * 2**20),
    )(selected, gram, filtered)


def gram_sum(gram, aside):
    half = gram.shape[0] // 2
    packed = jnp.concatenate([gram[:half, :half], gram[half:, :half], gram[half:, half:]], axis=0)
    chip = lax.all_gather(packed, "c").sum(axis=0)
    rows = packed.shape[0] // lax.axis_size("c")
    own = lax.dynamic_slice_in_dim(chip, lax.axis_index("c") * rows, rows, axis=0)
    plane = ("y", "x")
    depth = lax.axis_size(plane)
    share = exchanged(own.reshape(depth, rows // depth, half), plane).sum(axis=0)
    share, aside = lax.optimization_barrier((share, aside))
    share = gathered(share, "z").sum(axis=0)
    own = gathered(share, plane).reshape(own.shape)
    return lax.all_gather(own, "c").reshape(packed.shape), aside


def local(coarse_vectors, self_links, hop_links, basis, selected):
    start = reordered(coarse_vectors[0, 0, 0, 0])
    hops = hop_links[:, 0, 0, 0, 0]
    hop_x = hops[0].astype(jnp.float32)
    hop_y = hops[1].astype(jnp.float32)
    site = self_links[0, 0, 0, 0].astype(jnp.float32) + (hop_x + hop_x.T) + (hop_y + hop_y.T)
    width = site.shape[0]
    site_high = lax.reduce_precision(site, 8, 7)
    parts = [site_high.astype(jnp.bfloat16), (site - site_high).astype(jnp.bfloat16)]
    own = reordered(jnp.concatenate([*parts, hops[2], hops[3]], axis=0))
    site = own[:width].astype(jnp.float32) + own[width : 2 * width].astype(jnp.float32)
    above_z, above_t = own[2 * width : 3 * width], own[3 * width :]

    def halos(down_t, up_t, up_z, down_z):
        from_below_t = shifted_along(up_t, 1)
        from_above_t = shifted_along(down_t, -1)
        from_below_z = shifted(up_z, GZ, 1)
        from_above_z = shifted(down_z, GZ, -1)
        return from_below_t, from_above_t, from_below_z, from_above_z

    def product(halo, links):
        halo = jnp.concatenate(halo, axis=1)
        return jnp.dot(halo, links, preferred_element_type=jnp.float32)

    sent = start.astype(jnp.bfloat16)
    count = sent.shape[0]
    up_t = jnp.concatenate([sent, above_t.T], axis=0)
    up_z = jnp.concatenate([sent, above_z.T], axis=0)
    near_t, far_t, near_z, far_z = halos(sent, up_t, up_z, sent)
    around = jnp.concatenate([near_t[count:], above_t, near_z[count:], above_z], axis=0)
    halo = near_t[:count], far_t, near_z[:count], far_z

    earlier = start
    current = dot(start, site) + product(halo, around)
    site2 = 2.0 * site
    around2 = 2.0 * around
    for _ in range(DEG - 1):
        near = dot(current, site2) - earlier
        sent = current.astype(jnp.bfloat16)
        halo = halos(sent, sent, sent, sent)
        earlier, current = current, near + product(halo, around2)
    gram, filtered = gram_sum(dot_t(current, current), reordered(current))
    total = lax.axis_size(GZ) * lax.axis_size(TA) * start.shape[1]
    count = selected.shape[0]
    stacked = rebuild_rows(selected, gram, filtered, float(total) ** 0.5)
    rebuilt = jnp.dot(stacked, basis[0, 0, 0, 0], preferred_element_type=jnp.float32)
    return rebuilt.astype(jnp.bfloat16).reshape(1, 1, 1, 1, 2, count, basis.shape[-1])


def solution(mesh):
    fine = Mesh(mesh.devices.reshape(8, 2, 4, 12), ("y", "c", "x", "z"))
    in_specs = (
        P(GZ, TA, None, None, None, None),
        P(GZ, TA, None, None, None, None),
        P(None, GZ, TA, None, None, None, None),
        P(GZ, TA, None, None, None, None),
        P(),
    )
    out_specs = P(GZ, TA, None, None, None, None, None)
    return jax.shard_map(local, mesh=fine, in_specs=in_specs, out_specs=out_specs, check_vma=False)
```

```python
import functools

import jax
import jax.numpy as jnp
from jax import lax
from jax.experimental import pallas as pl
from jax.experimental.pallas import tpu as pltpu
from jax.sharding import Mesh, PartitionSpec as P

DEG = 16
HIGHEST = lax.Precision.HIGHEST
GZ = ("y", "c")
TA = ("x", "z")
TILE = 8
REST_ROWS = 16
REFINE_STEPS = 6
REFINE_ERROR = 1e-5


def shifted(value, axis, steps):
    count = lax.axis_size(axis)
    pairs = [(source, (source + steps) % count) for source in range(count)]
    return lax.ppermute(value, axis, pairs)


def along(site):
    rows, places = lax.axis_size("x"), lax.axis_size("z")
    row, place = divmod(site % (rows * places), places)
    return row * places + (place if row % 2 == 0 else places - 1 - place)


def reordered(value):
    pairs = [(site, along(site)) for site in range(lax.axis_size(TA))]
    return lax.ppermute(value, TA, pairs)


def shifted_along(value, steps):
    pairs = [(along(site), along(site + steps)) for site in range(lax.axis_size(TA))]
    return lax.ppermute(value, TA, pairs)


def exchanged(value, axis):
    return lax.all_to_all(value, axis, 0, 0, tiled=True)


def gathered(value, axis):
    count = lax.axis_size(axis)
    sent = jnp.broadcast_to(value[None], (count,) + value.shape)
    return exchanged(sent, axis)


def dot(left, right):
    return jnp.dot(left, right, precision=HIGHEST, preferred_element_type=jnp.float32)


def dot_t(left, right):
    return lax.dot_general(
        left,
        right,
        (((1,), (1,)), ((), ())),
        precision=HIGHEST,
        preferred_element_type=jnp.float32,
    )


def lower_inverse(matrix):
    size = matrix.shape[0]
    lane = lax.broadcasted_iota(jnp.int32, (TILE, size), 1)
    sublane = lax.broadcasted_iota(jnp.int32, (TILE, size), 0)
    groups = [matrix[g * TILE : (g + 1) * TILE, :] for g in range(size // TILE)]
    full = (TILE, size)
    for pivot in range(size):
        own, inner = divmod(pivot, TILE)
        row = jnp.broadcast_to(groups[own][inner : inner + 1, :], full)
        columns = {
            g: jnp.broadcast_to(groups[g][:, pivot : pivot + 1], full)
            for g in range(own, len(groups))
        }
        scale = 1.0 / jnp.broadcast_to(columns[own][inner : inner + 1, :], full)
        here = lane == pivot
        for g in range(own, len(groups)):
            factors = columns[g] * scale
            updated = jnp.where(here, -factors, groups[g] - factors * row)
            if g == own:
                updated = jnp.where(sublane > inner, updated, groups[g])
            groups[g] = updated
    result = []
    for g in range(len(groups)):
        rows = sublane + g * TILE
        diagonal = jnp.sum(jnp.where(lane == rows, groups[g], 0.0), axis=1, keepdims=True)
        unit = jnp.where(lane < rows, groups[g], jnp.where(lane == rows, 1.0, 0.0))
        result.append(unit * lax.rsqrt(diagonal))
    return jnp.concatenate(result, axis=0)


def split(value):
    high = value.astype(jnp.bfloat16)
    return high, (value - high.astype(jnp.float32)).astype(jnp.bfloat16)


def dot3(left, right, contract):
    dims = (((1,), (contract,)), ((), ()))
    (lh, ll), (rh, rl) = left, right
    one = functools.partial(
        lax.dot_general, dimension_numbers=dims, preferred_element_type=jnp.float32
    )
    return one(lh, rh) + (one(lh, rl) + one(ll, rh))


def select_kernel(scale, selected_ref, gram_ref, filtered_ref, out_ref, root_ref, picked_ref):
    size = root_ref.shape[0]
    half = size // 2
    first_block = gram_ref[0:half, :]
    cross_block = gram_ref[half : 2 * half, :]
    second_block = gram_ref[2 * half : 3 * half, :]
    gram = jnp.concatenate(
        [
            jnp.concatenate([first_block, cross_block.T], axis=1),
            jnp.concatenate([cross_block, second_block], axis=1),
        ],
        axis=0,
    )
    row = lax.broadcasted_iota(jnp.int32, gram.shape, 0)
    column = lax.broadcasted_iota(jnp.int32, gram.shape, 1)
    diagonal = jnp.where(row == column, gram, 0.0)
    across = lax.rsqrt(jnp.sum(diagonal, axis=0, keepdims=True))
    down = lax.rsqrt(jnp.sum(diagonal, axis=1, keepdims=True))
    scaled = gram * down * across
    scaled_parts = split(scaled)
    identity = jnp.where(row == column, 1.0, 0.0)
    root_ref[...] = jnp.where(row > column, -scaled, identity)

    def refine(state):
        step, _ = state
        root = split(root_ref[...])
        half_way = split(dot3(root, scaled_parts, 0))
        residual = dot3(half_way, root, 1) - identity
        lower = jnp.where(row > column, residual, 0.5 * identity * residual)
        root_ref[...] = root_ref[...] - dot3(split(lower), root, 0)
        return step + 1, jnp.sum(residual * residual)

    def unfinished(state):
        step, error = state
        return jnp.logical_and(step < REFINE_STEPS, error >= REFINE_ERROR)

    _, error = lax.while_loop(unfinished, refine, (jnp.int32(0), jnp.float32(1.0)))
    refined = error < REFINE_ERROR

    @pl.when(refined)
    def _():
        root_ref[...] = root_ref[...] * across

    @pl.when(jnp.logical_not(refined))
    def _():
        first = lower_inverse(gram_ref[0:half, :])
        below = dot_t(gram_ref[half : 2 * half, :], first)
        second = lower_inverse(gram_ref[2 * half : 3 * half, :] - dot_t(below, below))
        root_ref[0:half, 0:half] = first
        root_ref[0:half, half:size] = jnp.zeros((half, half), jnp.float32)
        root_ref[half:size, 0:half] = -dot(second, dot(below, first))
        root_ref[half:size, half:size] = second

    count = picked_ref.shape[0]
    for k in range(count):
        picked_ref[k : k + 1, :] = root_ref[pl.ds(selected_ref[k], 1), :]
    coefficients = dot(picked_ref[...] * scale, filtered_ref[...])
    coefficients = coefficients.astype(jnp.bfloat16).astype(jnp.float32)
    width = coefficients.shape[1]
    lane = lax.broadcasted_iota(jnp.int32, coefficients.shape, 1)
    out_ref[0:count, :] = jnp.where(lane < width // 2, coefficients, -coefficients).astype(
        jnp.bfloat16
    )
    swapped = jnp.concatenate(
        [coefficients[:, width // 2 :], coefficients[:, : width // 2]], axis=1
    )
    out_ref[count : 2 * count, :] = swapped.astype(jnp.bfloat16)


def rebuild_rows(selected, gram, filtered, scale):
    count = selected.shape[0]
    size, width = filtered.shape
    vmem = pl.BlockSpec(memory_space=pltpu.VMEM)
    return pl.pallas_call(
        functools.partial(select_kernel, scale),
        out_shape=jax.ShapeDtypeStruct((2 * count, width), jnp.bfloat16),
        in_specs=[pl.BlockSpec(memory_space=pltpu.SMEM), vmem, vmem],
        out_specs=vmem,
        scratch_shapes=[
            pltpu.VMEM((size, size), jnp.float32),
            pltpu.VMEM((count, size), jnp.float32),
        ],
        compiler_params=pltpu.CompilerParams(vmem_limit_bytes=16 * 2**20),
    )(selected, gram, filtered)


def gram_sum(gram):
    half = gram.shape[0] // 2
    packed = jnp.concatenate([gram[:half, :half], gram[half:, :half], gram[half:, half:]], axis=0)
    depth = lax.axis_size(GZ)
    share = exchanged(packed.reshape(depth, packed.shape[0] // depth, half), GZ).sum(axis=0)
    share = gathered(share, "x").sum(axis=0)
    share = gathered(share, "z").sum(axis=0)
    return gathered(share, GZ).reshape(packed.shape)


def packed_symmetric(matrix):
    high = lax.reduce_precision(matrix, 8, 7)
    low = matrix - high
    row = lax.broadcasted_iota(jnp.int32, matrix.shape, 0)
    column = lax.broadcasted_iota(jnp.int32, matrix.shape, 1)
    square = jnp.where(row >= column, high, low)
    rest = jnp.sum(jnp.where(row == column, low, 0.0), axis=0, keepdims=True)
    rest = jnp.broadcast_to(rest, (REST_ROWS, rest.shape[1]))
    return jnp.concatenate([square, rest], axis=0).astype(jnp.bfloat16)


def unpacked_symmetric(rows):
    rows = rows.astype(jnp.float32)
    size = rows.shape[1]
    square, rest = rows[:size], rows[size : size + 1]
    row = lax.broadcasted_iota(jnp.int32, square.shape, 0)
    column = lax.broadcasted_iota(jnp.int32, square.shape, 1)
    return square + jnp.where(row == column, rest, square.T)


def local(coarse_vectors, self_links, hop_links, basis, selected):
    sent = reordered(coarse_vectors[0, 0, 0, 0].astype(jnp.bfloat16))
    hops = hop_links[:, 0, 0, 0, 0]
    hop_x = hops[0].astype(jnp.float32)
    hop_y = hops[1].astype(jnp.float32)
    site = self_links[0, 0, 0, 0].astype(jnp.float32) + (hop_x + hop_x.T) + (hop_y + hop_y.T)
    width = site.shape[0]
    own = reordered(jnp.concatenate([hops[2], hops[3], packed_symmetric(site)], axis=0))
    above_z, above_t = own[:width], own[width : 2 * width]
    site = unpacked_symmetric(own[2 * width :])
    start = sent.astype(jnp.float32)

    def halos(down_t, up_t, up_z, down_z):
        from_below_t = shifted_along(up_t, 1)
        from_above_t = shifted_along(down_t, -1)
        from_below_z = shifted(up_z, GZ, 1)
        from_above_z = shifted(down_z, GZ, -1)
        return from_below_t, from_above_t, from_below_z, from_above_z

    def product(halo, links):
        halo = jnp.concatenate(halo, axis=1)
        return jnp.dot(halo, links, preferred_element_type=jnp.float32)

    up_t = jnp.concatenate([sent, above_t.T], axis=0)
    up_z = jnp.concatenate([sent, above_z.T], axis=0)
    count = sent.shape[0]
    near_t, far_t, near_z, far_z = halos(sent, up_t, up_z, sent)
    around = jnp.concatenate([near_t[count:], above_t, near_z[count:], above_z], axis=0)
    halo = near_t[:count], far_t, near_z[:count], far_z

    earlier = start
    current = dot(start, site) + product(halo, around)
    site2 = 2.0 * site
    around2 = 2.0 * around
    for _ in range(DEG - 1):
        near = dot(current, site2) - earlier
        sent = current.astype(jnp.bfloat16)
        halo = halos(sent, sent, sent, sent)
        earlier, current = current, near + product(halo, around2)
    filtered = reordered(current)

    gram = gram_sum(dot_t(current, current))
    total = lax.axis_size(GZ) * lax.axis_size(TA) * start.shape[1]
    count = selected.shape[0]
    stacked = rebuild_rows(selected, gram, filtered, float(total) ** 0.5)
    rebuilt = jnp.dot(stacked, basis[0, 0, 0, 0], preferred_element_type=jnp.float32)
    return rebuilt.astype(jnp.bfloat16).reshape(1, 1, 1, 1, 2, count, basis.shape[-1])


def solution(mesh):
    fine = Mesh(mesh.devices.reshape(8, 2, 4, 12), ("y", "c", "x", "z"))
    in_specs = (
        P(GZ, TA, None, None, None, None),
        P(GZ, TA, None, None, None, None),
        P(None, GZ, TA, None, None, None, None),
        P(GZ, TA, None, None, None, None),
        P(),
    )
    out_specs = P(GZ, TA, None, None, None, None, None)
    return jax.shard_map(local, mesh=fine, in_specs=in_specs, out_specs=out_specs, check_vma=False)
```

```python
import functools

import jax
import jax.numpy as jnp
from jax import lax
from jax.experimental import pallas as pl
from jax.experimental.pallas import tpu as pltpu
from jax.sharding import Mesh, PartitionSpec as P

DEG = 16
HIGHEST = lax.Precision.HIGHEST
GZ = ("y", "c")
TA = ("x", "z")
TILE = 8
REST_ROWS = 16
REFINE_STEPS = 6
REFINE_ERROR = 1e-5


def shifted(value, axis, steps):
    count = lax.axis_size(axis)
    pairs = [(source, (source + steps) % count) for source in range(count)]
    return lax.ppermute(value, axis, pairs)


def along(site):
    rows, places = lax.axis_size("x"), lax.axis_size("z")
    row, place = divmod(site % (rows * places), places)
    return row * places + (place if row % 2 == 0 else places - 1 - place)


def reordered(value):
    pairs = [(site, along(site)) for site in range(lax.axis_size(TA))]
    return lax.ppermute(value, TA, pairs)


def shifted_along(value, steps):
    pairs = [(along(site), along(site + steps)) for site in range(lax.axis_size(TA))]
    return lax.ppermute(value, TA, pairs)


def exchanged(value, axis):
    return lax.all_to_all(value, axis, 0, 0, tiled=True)


def gathered(value, axis):
    count = lax.axis_size(axis)
    sent = jnp.broadcast_to(value[None], (count,) + value.shape)
    return exchanged(sent, axis)


def dot(left, right):
    return jnp.dot(left, right, precision=HIGHEST, preferred_element_type=jnp.float32)


def dot_t(left, right):
    return lax.dot_general(
        left,
        right,
        (((1,), (1,)), ((), ())),
        precision=HIGHEST,
        preferred_element_type=jnp.float32,
    )


def lower_inverse(matrix):
    size = matrix.shape[0]
    lane = lax.broadcasted_iota(jnp.int32, (TILE, size), 1)
    sublane = lax.broadcasted_iota(jnp.int32, (TILE, size), 0)
    groups = [matrix[g * TILE : (g + 1) * TILE, :] for g in range(size // TILE)]
    full = (TILE, size)
    for pivot in range(size):
        own, inner = divmod(pivot, TILE)
        row = jnp.broadcast_to(groups[own][inner : inner + 1, :], full)
        columns = {
            g: jnp.broadcast_to(groups[g][:, pivot : pivot + 1], full)
            for g in range(own, len(groups))
        }
        scale = 1.0 / jnp.broadcast_to(columns[own][inner : inner + 1, :], full)
        here = lane == pivot
        for g in range(own, len(groups)):
            factors = columns[g] * scale
            updated = jnp.where(here, -factors, groups[g] - factors * row)
            if g == own:
                updated = jnp.where(sublane > inner, updated, groups[g])
            groups[g] = updated
    result = []
    for g in range(len(groups)):
        rows = sublane + g * TILE
        diagonal = jnp.sum(jnp.where(lane == rows, groups[g], 0.0), axis=1, keepdims=True)
        unit = jnp.where(lane < rows, groups[g], jnp.where(lane == rows, 1.0, 0.0))
        result.append(unit * lax.rsqrt(diagonal))
    return jnp.concatenate(result, axis=0)


def split(value):
    high = value.astype(jnp.bfloat16)
    return high, (value - high.astype(jnp.float32)).astype(jnp.bfloat16)


def dot3(left, right, contract):
    dims = (((1,), (contract,)), ((), ()))
    (lh, ll), (rh, rl) = left, right
    one = functools.partial(
        lax.dot_general, dimension_numbers=dims, preferred_element_type=jnp.float32
    )
    return one(lh, rh) + (one(lh, rl) + one(ll, rh))


def select_kernel(scale, selected_ref, gram_ref, filtered_ref, out_ref, root_ref, picked_ref):
    size = root_ref.shape[0]
    half = size // 2
    first_block = gram_ref[0:half, :]
    cross_block = gram_ref[half : 2 * half, :]
    second_block = gram_ref[2 * half : 3 * half, :]
    gram = jnp.concatenate(
        [
            jnp.concatenate([first_block, cross_block.T], axis=1),
            jnp.concatenate([cross_block, second_block], axis=1),
        ],
        axis=0,
    )
    row = lax.broadcasted_iota(jnp.int32, gram.shape, 0)
    column = lax.broadcasted_iota(jnp.int32, gram.shape, 1)
    diagonal = jnp.where(row == column, gram, 0.0)
    across = lax.rsqrt(jnp.sum(diagonal, axis=0, keepdims=True))
    down = lax.rsqrt(jnp.sum(diagonal, axis=1, keepdims=True))
    scaled = gram * down * across
    scaled_parts = split(scaled)
    identity = jnp.where(row == column, 1.0, 0.0)
    root_ref[...] = jnp.where(row > column, -scaled, identity)

    def refine(state):
        step, _ = state
        root = split(root_ref[...])
        half_way = split(dot3(root, scaled_parts, 0))
        residual = dot3(half_way, root, 1) - identity
        lower = jnp.where(row > column, residual, 0.5 * identity * residual)
        root_ref[...] = root_ref[...] - dot3(split(lower), root, 0)
        return step + 1, jnp.sum(residual * residual)

    def unfinished(state):
        step, error = state
        return jnp.logical_and(step < REFINE_STEPS, error >= REFINE_ERROR)

    _, error = lax.while_loop(unfinished, refine, (jnp.int32(0), jnp.float32(1.0)))
    refined = error < REFINE_ERROR

    @pl.when(refined)
    def _():
        root_ref[...] = root_ref[...] * across

    @pl.when(jnp.logical_not(refined))
    def _():
        first = lower_inverse(gram_ref[0:half, :])
        below = dot_t(gram_ref[half : 2 * half, :], first)
        second = lower_inverse(gram_ref[2 * half : 3 * half, :] - dot_t(below, below))
        root_ref[0:half, 0:half] = first
        root_ref[0:half, half:size] = jnp.zeros((half, half), jnp.float32)
        root_ref[half:size, 0:half] = -dot(second, dot(below, first))
        root_ref[half:size, half:size] = second

    count = picked_ref.shape[0]
    for k in range(count):
        picked_ref[k : k + 1, :] = root_ref[pl.ds(selected_ref[k], 1), :]
    coefficients = dot(picked_ref[...] * scale, filtered_ref[...].astype(jnp.float32))
    coefficients = coefficients.astype(jnp.bfloat16).astype(jnp.float32)
    width = coefficients.shape[1]
    lane = lax.broadcasted_iota(jnp.int32, coefficients.shape, 1)
    out_ref[0:count, :] = jnp.where(lane < width // 2, coefficients, -coefficients).astype(
        jnp.bfloat16
    )
    swapped = jnp.concatenate(
        [coefficients[:, width // 2 :], coefficients[:, : width // 2]], axis=1
    )
    out_ref[count : 2 * count, :] = swapped.astype(jnp.bfloat16)


def rebuild_rows(selected, gram, filtered, scale):
    count = selected.shape[0]
    size, width = filtered.shape
    vmem = pl.BlockSpec(memory_space=pltpu.VMEM)
    return pl.pallas_call(
        functools.partial(select_kernel, scale),
        out_shape=jax.ShapeDtypeStruct((2 * count, width), jnp.bfloat16),
        in_specs=[pl.BlockSpec(memory_space=pltpu.SMEM), vmem, vmem],
        out_specs=vmem,
        scratch_shapes=[
            pltpu.VMEM((size, size), jnp.float32),
            pltpu.VMEM((count, size), jnp.float32),
        ],
        compiler_params=pltpu.CompilerParams(vmem_limit_bytes=16 * 2**20),
    )(selected, gram, filtered)


def gram_sum(gram, aside):
    half = gram.shape[0] // 2
    packed = jnp.concatenate([gram[:half, :half], gram[half:, :half], gram[half:, half:]], axis=0)
    depth = lax.axis_size(GZ)
    share = exchanged(packed.reshape(depth, packed.shape[0] // depth, half), GZ).sum(axis=0)
    share, aside = lax.optimization_barrier((share, aside))
    share = gathered(share, "x").sum(axis=0)
    share = gathered(share, "z").sum(axis=0)
    return gathered(share, GZ).reshape(packed.shape), aside


def packed_symmetric(matrix):
    high = lax.reduce_precision(matrix, 8, 7)
    low = matrix - high
    row = lax.broadcasted_iota(jnp.int32, matrix.shape, 0)
    column = lax.broadcasted_iota(jnp.int32, matrix.shape, 1)
    square = jnp.where(row >= column, high, low)
    rest = jnp.sum(jnp.where(row == column, low, 0.0), axis=0, keepdims=True)
    rest = jnp.broadcast_to(rest, (REST_ROWS, rest.shape[1]))
    return jnp.concatenate([square, rest], axis=0).astype(jnp.bfloat16)


def unpacked_symmetric(rows):
    rows = rows.astype(jnp.float32)
    size = rows.shape[1]
    square, rest = rows[:size], rows[size : size + 1]
    row = lax.broadcasted_iota(jnp.int32, square.shape, 0)
    column = lax.broadcasted_iota(jnp.int32, square.shape, 1)
    return square + jnp.where(row == column, rest, square.T)


def local(coarse_vectors, self_links, hop_links, basis, selected):
    sent = reordered(coarse_vectors[0, 0, 0, 0].astype(jnp.bfloat16))
    hops = hop_links[:, 0, 0, 0, 0]
    hop_x = hops[0].astype(jnp.float32)
    hop_y = hops[1].astype(jnp.float32)
    site = self_links[0, 0, 0, 0].astype(jnp.float32) + (hop_x + hop_x.T) + (hop_y + hop_y.T)
    width = site.shape[0]
    own = reordered(jnp.concatenate([hops[2], hops[3], packed_symmetric(site)], axis=0))
    above_z, above_t = own[:width], own[width : 2 * width]
    site = unpacked_symmetric(own[2 * width :])
    start = sent.astype(jnp.float32)

    def halos(down_t, up_t, up_z, down_z):
        from_below_t = shifted_along(up_t, 1)
        from_above_t = shifted_along(down_t, -1)
        from_below_z = shifted(up_z, GZ, 1)
        from_above_z = shifted(down_z, GZ, -1)
        return from_below_t, from_above_t, from_below_z, from_above_z

    def product(halo, links):
        halo = jnp.concatenate(halo, axis=1)
        return jnp.dot(halo, links, preferred_element_type=jnp.float32)

    up_t = jnp.concatenate([sent, above_t.T], axis=0)
    up_z = jnp.concatenate([sent, above_z.T], axis=0)
    count = sent.shape[0]
    near_t, far_t, near_z, far_z = halos(sent, up_t, up_z, sent)
    around = jnp.concatenate([near_t[count:], above_t, near_z[count:], above_z], axis=0)
    halo = near_t[:count], far_t, near_z[:count], far_z

    earlier = start
    current = dot(start, site) + product(halo, around)
    site2 = 2.0 * site
    around2 = 2.0 * around
    for _ in range(DEG - 1):
        near = dot(current, site2) - earlier
        sent = current.astype(jnp.bfloat16)
        halo = halos(sent, sent, sent, sent)
        earlier, current = current, near + product(halo, around2)
    gram, filtered = gram_sum(dot_t(current, current), reordered(current.astype(jnp.bfloat16)))
    total = lax.axis_size(GZ) * lax.axis_size(TA) * start.shape[1]
    count = selected.shape[0]
    stacked = rebuild_rows(selected, gram, filtered, float(total) ** 0.5)
    rebuilt = jnp.dot(stacked, basis[0, 0, 0, 0], preferred_element_type=jnp.float32)
    return rebuilt.astype(jnp.bfloat16).reshape(1, 1, 1, 1, 2, count, basis.shape[-1])


def solution(mesh):
    fine = Mesh(mesh.devices.reshape(8, 2, 4, 12), ("y", "c", "x", "z"))
    in_specs = (
        P(GZ, TA, None, None, None, None),
        P(GZ, TA, None, None, None, None),
        P(None, GZ, TA, None, None, None, None),
        P(GZ, TA, None, None, None, None),
        P(),
    )
    out_specs = P(GZ, TA, None, None, None, None, None)
    return jax.shard_map(local, mesh=fine, in_specs=in_specs, out_specs=out_specs, check_vma=False)
```

```python
import functools

import jax
import jax.numpy as jnp
from jax import lax
from jax.experimental import pallas as pl
from jax.experimental.pallas import tpu as pltpu
from jax.sharding import Mesh, PartitionSpec as P

DEG = 16
HIGHEST = lax.Precision.HIGHEST
GZ = ("y", "c")
TA = ("x", "z")
TILE = 8
REST_ROWS = 16
REFINE_STEPS = 6
REFINE_ERROR = 1e-5


def shifted(value, axis, steps):
    count = lax.axis_size(axis)
    pairs = [(source, (source + steps) % count) for source in range(count)]
    return lax.ppermute(value, axis, pairs)


def along(site):
    rows, places = lax.axis_size("x"), lax.axis_size("z")
    row, place = divmod(site % (rows * places), places)
    return row * places + (place if row % 2 == 0 else places - 1 - place)


def reordered(value):
    pairs = [(site, along(site)) for site in range(lax.axis_size(TA))]
    return lax.ppermute(value, TA, pairs)


def shifted_along(value, steps):
    pairs = [(along(site), along(site + steps)) for site in range(lax.axis_size(TA))]
    return lax.ppermute(value, TA, pairs)


def exchanged(value, axis):
    return lax.all_to_all(value, axis, 0, 0, tiled=True)


def gathered(value, axis):
    count = lax.axis_size(axis)
    sent = jnp.broadcast_to(value[None], (count,) + value.shape)
    return exchanged(sent, axis)


def dot(left, right):
    return jnp.dot(left, right, precision=HIGHEST, preferred_element_type=jnp.float32)


def dot_t(left, right):
    return lax.dot_general(
        left,
        right,
        (((1,), (1,)), ((), ())),
        precision=HIGHEST,
        preferred_element_type=jnp.float32,
    )


def lower_inverse(matrix):
    size = matrix.shape[0]
    lane = lax.broadcasted_iota(jnp.int32, (TILE, size), 1)
    sublane = lax.broadcasted_iota(jnp.int32, (TILE, size), 0)
    groups = [matrix[g * TILE : (g + 1) * TILE, :] for g in range(size // TILE)]
    full = (TILE, size)
    for pivot in range(size):
        own, inner = divmod(pivot, TILE)
        row = jnp.broadcast_to(groups[own][inner : inner + 1, :], full)
        columns = {
            g: jnp.broadcast_to(groups[g][:, pivot : pivot + 1], full)
            for g in range(own, len(groups))
        }
        scale = 1.0 / jnp.broadcast_to(columns[own][inner : inner + 1, :], full)
        here = lane == pivot
        for g in range(own, len(groups)):
            factors = columns[g] * scale
            updated = jnp.where(here, -factors, groups[g] - factors * row)
            if g == own:
                updated = jnp.where(sublane > inner, updated, groups[g])
            groups[g] = updated
    result = []
    for g in range(len(groups)):
        rows = sublane + g * TILE
        diagonal = jnp.sum(jnp.where(lane == rows, groups[g], 0.0), axis=1, keepdims=True)
        unit = jnp.where(lane < rows, groups[g], jnp.where(lane == rows, 1.0, 0.0))
        result.append(unit * lax.rsqrt(diagonal))
    return jnp.concatenate(result, axis=0)


def split(value):
    high = value.astype(jnp.bfloat16)
    return high, (value - high.astype(jnp.float32)).astype(jnp.bfloat16)


def dot3(left, right, contract):
    dims = (((1,), (contract,)), ((), ()))
    (lh, ll), (rh, rl) = left, right
    one = functools.partial(
        lax.dot_general, dimension_numbers=dims, preferred_element_type=jnp.float32
    )
    return one(lh, rh) + (one(lh, rl) + one(ll, rh))


def select_kernel(scale, selected_ref, gram_ref, filtered_ref, out_ref, root_ref, picked_ref):
    size = root_ref.shape[0]
    half = size // 2
    first_block = gram_ref[0:half, :]
    cross_block = gram_ref[half : 2 * half, :]
    second_block = gram_ref[2 * half : 3 * half, :]
    gram = jnp.concatenate(
        [
            jnp.concatenate([first_block, cross_block.T], axis=1),
            jnp.concatenate([cross_block, second_block], axis=1),
        ],
        axis=0,
    )
    row = lax.broadcasted_iota(jnp.int32, gram.shape, 0)
    column = lax.broadcasted_iota(jnp.int32, gram.shape, 1)
    diagonal = jnp.where(row == column, gram, 0.0)
    across = lax.rsqrt(jnp.sum(diagonal, axis=0, keepdims=True))
    down = lax.rsqrt(jnp.sum(diagonal, axis=1, keepdims=True))
    scaled = gram * down * across
    scaled_parts = split(scaled)
    identity = jnp.where(row == column, 1.0, 0.0)
    root_ref[...] = jnp.where(row > column, -scaled, identity)

    def refine(state):
        step, _ = state
        root = split(root_ref[...])
        half_way = split(dot3(root, scaled_parts, 0))
        residual = dot3(half_way, root, 1) - identity
        lower = jnp.where(row > column, residual, 0.5 * identity * residual)
        root_ref[...] = root_ref[...] - dot3(split(lower), root, 0)
        return step + 1, jnp.sum(residual * residual)

    def unfinished(state):
        step, error = state
        return jnp.logical_and(step < REFINE_STEPS, error >= REFINE_ERROR)

    _, error = lax.while_loop(unfinished, refine, (jnp.int32(0), jnp.float32(1.0)))
    refined = error < REFINE_ERROR

    @pl.when(refined)
    def _():
        root_ref[...] = root_ref[...] * across

    @pl.when(jnp.logical_not(refined))
    def _():
        first = lower_inverse(gram_ref[0:half, :])
        below = dot_t(gram_ref[half : 2 * half, :], first)
        second = lower_inverse(gram_ref[2 * half : 3 * half, :] - dot_t(below, below))
        root_ref[0:half, 0:half] = first
        root_ref[0:half, half:size] = jnp.zeros((half, half), jnp.float32)
        root_ref[half:size, 0:half] = -dot(second, dot(below, first))
        root_ref[half:size, half:size] = second

    count = picked_ref.shape[0]
    for k in range(count):
        picked_ref[k : k + 1, :] = root_ref[pl.ds(selected_ref[k], 1), :]
    coefficients = dot(picked_ref[...] * scale, filtered_ref[...])
    coefficients = coefficients.astype(jnp.bfloat16).astype(jnp.float32)
    width = coefficients.shape[1]
    lane = lax.broadcasted_iota(jnp.int32, coefficients.shape, 1)
    out_ref[0:count, :] = jnp.where(lane < width // 2, coefficients, -coefficients).astype(
        jnp.bfloat16
    )
    swapped = jnp.concatenate(
        [coefficients[:, width // 2 :], coefficients[:, : width // 2]], axis=1
    )
    out_ref[count : 2 * count, :] = swapped.astype(jnp.bfloat16)


def rebuild_rows(selected, gram, filtered, scale):
    count = selected.shape[0]
    size, width = filtered.shape
    vmem = pl.BlockSpec(memory_space=pltpu.VMEM)
    return pl.pallas_call(
        functools.partial(select_kernel, scale),
        out_shape=jax.ShapeDtypeStruct((2 * count, width), jnp.bfloat16),
        in_specs=[pl.BlockSpec(memory_space=pltpu.SMEM), vmem, vmem],
        out_specs=vmem,
        scratch_shapes=[
            pltpu.VMEM((size, size), jnp.float32),
            pltpu.VMEM((count, size), jnp.float32),
        ],
        compiler_params=pltpu.CompilerParams(vmem_limit_bytes=16 * 2**20),
    )(selected, gram, filtered)


def gram_sum(gram, aside):
    half = gram.shape[0] // 2
    packed = jnp.concatenate([gram[:half, :half], gram[half:, :half], gram[half:, half:]], axis=0)
    depth = lax.axis_size(GZ)
    share = exchanged(packed.reshape(depth, packed.shape[0] // depth, half), GZ).sum(axis=0)
    share, aside = lax.optimization_barrier((share, aside))
    share = gathered(share, "x").sum(axis=0)
    share = gathered(share, "z").sum(axis=0)
    share, aside = lax.optimization_barrier((share, aside))
    return gathered(share, GZ).reshape(packed.shape), aside.astype(jnp.float32)


def packed_symmetric(matrix):
    high = lax.reduce_precision(matrix, 8, 7)
    low = matrix - high
    row = lax.broadcasted_iota(jnp.int32, matrix.shape, 0)
    column = lax.broadcasted_iota(jnp.int32, matrix.shape, 1)
    square = jnp.where(row >= column, high, low)
    rest = jnp.sum(jnp.where(row == column, low, 0.0), axis=0, keepdims=True)
    rest = jnp.broadcast_to(rest, (REST_ROWS, rest.shape[1]))
    return jnp.concatenate([square, rest], axis=0).astype(jnp.bfloat16)


def unpacked_symmetric(rows):
    rows = rows.astype(jnp.float32)
    size = rows.shape[1]
    square, rest = rows[:size], rows[size : size + 1]
    row = lax.broadcasted_iota(jnp.int32, square.shape, 0)
    column = lax.broadcasted_iota(jnp.int32, square.shape, 1)
    return square + jnp.where(row == column, rest, square.T)


def local(coarse_vectors, self_links, hop_links, basis, selected):
    sent = reordered(coarse_vectors[0, 0, 0, 0].astype(jnp.bfloat16))
    hops = hop_links[:, 0, 0, 0, 0]
    hop_x = hops[0].astype(jnp.float32)
    hop_y = hops[1].astype(jnp.float32)
    site = self_links[0, 0, 0, 0].astype(jnp.float32) + (hop_x + hop_x.T) + (hop_y + hop_y.T)
    width = site.shape[0]
    own = reordered(jnp.concatenate([hops[2], hops[3], packed_symmetric(site)], axis=0))
    above_z, above_t = own[:width], own[width : 2 * width]
    site = unpacked_symmetric(own[2 * width :])
    start = sent.astype(jnp.float32)

    def halos(down_t, up_t, up_z, down_z):
        from_below_t = shifted_along(up_t, 1)
        from_above_t = shifted_along(down_t, -1)
        from_below_z = shifted(up_z, GZ, 1)
        from_above_z = shifted(down_z, GZ, -1)
        return from_below_t, from_above_t, from_below_z, from_above_z

    def product(halo, links):
        halo = jnp.concatenate(halo, axis=1)
        return jnp.dot(halo, links, preferred_element_type=jnp.float32)

    up_t = jnp.concatenate([sent, above_t.T], axis=0)
    up_z = jnp.concatenate([sent, above_z.T], axis=0)
    count = sent.shape[0]
    near_t, far_t, near_z, far_z = halos(sent, up_t, up_z, sent)
    around = jnp.concatenate([near_t[count:], above_t, near_z[count:], above_z], axis=0)
    halo = near_t[:count], far_t, near_z[:count], far_z

    earlier = start
    current = dot(start, site) + product(halo, around)
    site2 = 2.0 * site
    around2 = 2.0 * around
    for _ in range(DEG - 1):
        near = dot(current, site2) - earlier
        sent = current.astype(jnp.bfloat16)
        halo = halos(sent, sent, sent, sent)
        earlier, current = current, near + product(halo, around2)
    gram, filtered = gram_sum(dot_t(current, current), reordered(current.astype(jnp.bfloat16)))
    total = lax.axis_size(GZ) * lax.axis_size(TA) * start.shape[1]
    count = selected.shape[0]
    stacked = rebuild_rows(selected, gram, filtered, float(total) ** 0.5)
    rebuilt = jnp.dot(stacked, basis[0, 0, 0, 0], preferred_element_type=jnp.float32)
    return rebuilt.astype(jnp.bfloat16).reshape(1, 1, 1, 1, 2, count, basis.shape[-1])


def solution(mesh):
    fine = Mesh(mesh.devices.reshape(8, 2, 4, 12), ("y", "c", "x", "z"))
    in_specs = (
        P(GZ, TA, None, None, None, None),
        P(GZ, TA, None, None, None, None),
        P(None, GZ, TA, None, None, None, None),
        P(GZ, TA, None, None, None, None),
        P(),
    )
    out_specs = P(GZ, TA, None, None, None, None, None)
    return jax.shard_map(local, mesh=fine, in_specs=in_specs, out_specs=out_specs, check_vma=False)
```

```python
import functools

import jax
import jax.numpy as jnp
from jax import lax
from jax.experimental import pallas as pl
from jax.experimental.pallas import tpu as pltpu
from jax.sharding import Mesh, PartitionSpec as P

DEG = 16
HIGHEST = lax.Precision.HIGHEST
GZ = ("y", "c")
TA = ("x", "z")
TILE = 8
REST_ROWS = 16
REFINE_STEPS = 6
REFINE_ERROR = 1e-5


def shifted(value, axis, steps):
    count = lax.axis_size(axis)
    pairs = [(source, (source + steps) % count) for source in range(count)]
    return lax.ppermute(value, axis, pairs)


def along(site):
    rows, places = lax.axis_size("x"), lax.axis_size("z")
    row, place = divmod(site % (rows * places), places)
    return row * places + (place if row % 2 == 0 else places - 1 - place)


def reordered(value):
    pairs = [(site, along(site)) for site in range(lax.axis_size(TA))]
    return lax.ppermute(value, TA, pairs)


def shifted_along(value, steps):
    pairs = [(along(site), along(site + steps)) for site in range(lax.axis_size(TA))]
    return lax.ppermute(value, TA, pairs)


def exchanged(value, axis):
    return lax.all_to_all(value, axis, 0, 0, tiled=True)


def gathered(value, axis):
    count = lax.axis_size(axis)
    sent = jnp.broadcast_to(value[None], (count,) + value.shape)
    return exchanged(sent, axis)


def dot(left, right):
    return jnp.dot(left, right, precision=HIGHEST, preferred_element_type=jnp.float32)


def dot_t(left, right):
    return lax.dot_general(
        left,
        right,
        (((1,), (1,)), ((), ())),
        precision=HIGHEST,
        preferred_element_type=jnp.float32,
    )


def lower_inverse(matrix):
    size = matrix.shape[0]
    lane = lax.broadcasted_iota(jnp.int32, (TILE, size), 1)
    sublane = lax.broadcasted_iota(jnp.int32, (TILE, size), 0)
    groups = [matrix[g * TILE : (g + 1) * TILE, :] for g in range(size // TILE)]
    full = (TILE, size)
    for pivot in range(size):
        own, inner = divmod(pivot, TILE)
        row = jnp.broadcast_to(groups[own][inner : inner + 1, :], full)
        columns = {
            g: jnp.broadcast_to(groups[g][:, pivot : pivot + 1], full)
            for g in range(own, len(groups))
        }
        scale = 1.0 / jnp.broadcast_to(columns[own][inner : inner + 1, :], full)
        here = lane == pivot
        for g in range(own, len(groups)):
            factors = columns[g] * scale
            updated = jnp.where(here, -factors, groups[g] - factors * row)
            if g == own:
                updated = jnp.where(sublane > inner, updated, groups[g])
            groups[g] = updated
    result = []
    for g in range(len(groups)):
        rows = sublane + g * TILE
        diagonal = jnp.sum(jnp.where(lane == rows, groups[g], 0.0), axis=1, keepdims=True)
        unit = jnp.where(lane < rows, groups[g], jnp.where(lane == rows, 1.0, 0.0))
        result.append(unit * lax.rsqrt(diagonal))
    return jnp.concatenate(result, axis=0)


def split(value):
    high = value.astype(jnp.bfloat16)
    return high, (value - high.astype(jnp.float32)).astype(jnp.bfloat16)


def dot3(left, right, contract):
    dims = (((1,), (contract,)), ((), ()))
    (lh, ll), (rh, rl) = left, right
    one = functools.partial(
        lax.dot_general, dimension_numbers=dims, preferred_element_type=jnp.float32
    )
    return one(lh, rh) + (one(lh, rl) + one(ll, rh))


def select_kernel(scale, selected_ref, gram_ref, filtered_ref, out_ref, root_ref, picked_ref):
    size = root_ref.shape[0]
    half = size // 2
    first_block = gram_ref[0:half, :]
    cross_block = gram_ref[half : 2 * half, :]
    second_block = gram_ref[2 * half : 3 * half, :]
    gram = jnp.concatenate(
        [
            jnp.concatenate([first_block, cross_block.T], axis=1),
            jnp.concatenate([cross_block, second_block], axis=1),
        ],
        axis=0,
    )
    row = lax.broadcasted_iota(jnp.int32, gram.shape, 0)
    column = lax.broadcasted_iota(jnp.int32, gram.shape, 1)
    diagonal = jnp.where(row == column, gram, 0.0)
    across = lax.rsqrt(jnp.sum(diagonal, axis=0, keepdims=True))
    down = lax.rsqrt(jnp.sum(diagonal, axis=1, keepdims=True))
    scaled = gram * down * across
    scaled_parts = split(scaled)
    identity = jnp.where(row == column, 1.0, 0.0)
    root_ref[...] = jnp.where(row > column, -scaled, identity)

    def refine(state):
        step, _ = state
        root = split(root_ref[...])
        half_way = split(dot3(root, scaled_parts, 0))
        residual = dot3(half_way, root, 1) - identity
        lower = jnp.where(row > column, residual, 0.5 * identity * residual)
        root_ref[...] = root_ref[...] - dot3(split(lower), root, 0)
        return step + 1, jnp.sum(residual * residual)

    def unfinished(state):
        step, error = state
        return jnp.logical_and(step < REFINE_STEPS, error >= REFINE_ERROR)

    _, error = lax.while_loop(unfinished, refine, (jnp.int32(0), jnp.float32(1.0)))
    refined = error < REFINE_ERROR

    @pl.when(refined)
    def _():
        root_ref[...] = root_ref[...] * across

    @pl.when(jnp.logical_not(refined))
    def _():
        first = lower_inverse(gram_ref[0:half, :])
        below = dot_t(gram_ref[half : 2 * half, :], first)
        second = lower_inverse(gram_ref[2 * half : 3 * half, :] - dot_t(below, below))
        root_ref[0:half, 0:half] = first
        root_ref[0:half, half:size] = jnp.zeros((half, half), jnp.float32)
        root_ref[half:size, 0:half] = -dot(second, dot(below, first))
        root_ref[half:size, half:size] = second

    count = picked_ref.shape[0]
    for k in range(count):
        picked_ref[k : k + 1, :] = root_ref[pl.ds(selected_ref[k], 1), :]
    coefficients = dot(picked_ref[...] * scale, filtered_ref[...].astype(jnp.float32))
    coefficients = coefficients.astype(jnp.bfloat16).astype(jnp.float32)
    width = coefficients.shape[1]
    lane = lax.broadcasted_iota(jnp.int32, coefficients.shape, 1)
    out_ref[0:count, :] = jnp.where(lane < width // 2, coefficients, -coefficients).astype(
        jnp.bfloat16
    )
    swapped = jnp.concatenate(
        [coefficients[:, width // 2 :], coefficients[:, : width // 2]], axis=1
    )
    out_ref[count : 2 * count, :] = swapped.astype(jnp.bfloat16)


def rebuild_rows(selected, gram, filtered, scale):
    count = selected.shape[0]
    size, width = filtered.shape
    vmem = pl.BlockSpec(memory_space=pltpu.VMEM)
    return pl.pallas_call(
        functools.partial(select_kernel, scale),
        out_shape=jax.ShapeDtypeStruct((2 * count, width), jnp.bfloat16),
        in_specs=[pl.BlockSpec(memory_space=pltpu.SMEM), vmem, vmem],
        out_specs=vmem,
        scratch_shapes=[
            pltpu.VMEM((size, size), jnp.float32),
            pltpu.VMEM((count, size), jnp.float32),
        ],
        compiler_params=pltpu.CompilerParams(vmem_limit_bytes=16 * 2**20),
    )(selected, gram, filtered)


def gram_sum(gram, aside):
    half = gram.shape[0] // 2
    packed = jnp.concatenate([gram[:half, :half], gram[half:, :half], gram[half:, half:]], axis=0)
    depth = lax.axis_size(GZ)
    share = exchanged(packed.reshape(depth, packed.shape[0] // depth, half), GZ).sum(axis=0)
    share = gathered(share, "x").sum(axis=0)
    share = gathered(share, "z").sum(axis=0)
    share, aside = lax.optimization_barrier((share, aside))
    return gathered(share, GZ).reshape(packed.shape), aside


def packed_symmetric(matrix):
    high = lax.reduce_precision(matrix, 8, 7)
    low = matrix - high
    row = lax.broadcasted_iota(jnp.int32, matrix.shape, 0)
    column = lax.broadcasted_iota(jnp.int32, matrix.shape, 1)
    square = jnp.where(row >= column, high, low)
    rest = jnp.sum(jnp.where(row == column, low, 0.0), axis=0, keepdims=True)
    rest = jnp.broadcast_to(rest, (REST_ROWS, rest.shape[1]))
    return jnp.concatenate([square, rest], axis=0).astype(jnp.bfloat16)


def unpacked_symmetric(rows):
    rows = rows.astype(jnp.float32)
    size = rows.shape[1]
    square, rest = rows[:size], rows[size : size + 1]
    row = lax.broadcasted_iota(jnp.int32, square.shape, 0)
    column = lax.broadcasted_iota(jnp.int32, square.shape, 1)
    return square + jnp.where(row == column, rest, square.T)


def local(coarse_vectors, self_links, hop_links, basis, selected):
    sent = reordered(coarse_vectors[0, 0, 0, 0].astype(jnp.bfloat16))
    hops = hop_links[:, 0, 0, 0, 0]
    hop_x = hops[0].astype(jnp.float32)
    hop_y = hops[1].astype(jnp.float32)
    site = self_links[0, 0, 0, 0].astype(jnp.float32) + (hop_x + hop_x.T) + (hop_y + hop_y.T)
    width = site.shape[0]
    own = reordered(jnp.concatenate([hops[2], hops[3], packed_symmetric(site)], axis=0))
    above_z, above_t = own[:width], own[width : 2 * width]
    site = unpacked_symmetric(own[2 * width :])
    start = sent.astype(jnp.float32)

    def halos(down_t, up_t, up_z, down_z):
        from_below_t = shifted_along(up_t, 1)
        from_above_t = shifted_along(down_t, -1)
        from_below_z = shifted(up_z, GZ, 1)
        from_above_z = shifted(down_z, GZ, -1)
        return from_below_t, from_above_t, from_below_z, from_above_z

    def product(halo, links):
        halo = jnp.concatenate(halo, axis=1)
        return jnp.dot(halo, links, preferred_element_type=jnp.float32)

    up_t = jnp.concatenate([sent, above_t.T], axis=0)
    up_z = jnp.concatenate([sent, above_z.T], axis=0)
    count = sent.shape[0]
    near_t, far_t, near_z, far_z = halos(sent, up_t, up_z, sent)
    around = jnp.concatenate([near_t[count:], above_t, near_z[count:], above_z], axis=0)
    halo = near_t[:count], far_t, near_z[:count], far_z

    earlier = start
    current = dot(start, site) + product(halo, around)
    site2 = 2.0 * site
    around2 = 2.0 * around
    for _ in range(DEG - 1):
        near = dot(current, site2) - earlier
        sent = current.astype(jnp.bfloat16)
        halo = halos(sent, sent, sent, sent)
        earlier, current = current, near + product(halo, around2)
    gram, filtered = gram_sum(dot_t(current, current), reordered(current.astype(jnp.bfloat16)))
    total = lax.axis_size(GZ) * lax.axis_size(TA) * start.shape[1]
    count = selected.shape[0]
    stacked = rebuild_rows(selected, gram, filtered, float(total) ** 0.5)
    rebuilt = jnp.dot(stacked, basis[0, 0, 0, 0], preferred_element_type=jnp.float32)
    return rebuilt.astype(jnp.bfloat16).reshape(1, 1, 1, 1, 2, count, basis.shape[-1])


def solution(mesh):
    fine = Mesh(mesh.devices.reshape(8, 2, 4, 12), ("y", "c", "x", "z"))
    in_specs = (
        P(GZ, TA, None, None, None, None),
        P(GZ, TA, None, None, None, None),
        P(None, GZ, TA, None, None, None, None),
        P(GZ, TA, None, None, None, None),
        P(),
    )
    out_specs = P(GZ, TA, None, None, None, None, None)
    return jax.shard_map(local, mesh=fine, in_specs=in_specs, out_specs=out_specs, check_vma=False)
```

```python
import functools

import jax
import jax.numpy as jnp
from jax import lax
from jax.experimental import pallas as pl
from jax.experimental.pallas import tpu as pltpu
from jax.sharding import Mesh, PartitionSpec as P

DEG = 16
HIGHEST = lax.Precision.HIGHEST
GZ = ("y", "c")
TA = ("x", "z")
TILE = 8
REST_ROWS = 16
REFINE_STEPS = 6
REFINE_ERROR = 1e-5


def shifted(value, axis, steps):
    count = lax.axis_size(axis)
    pairs = [(source, (source + steps) % count) for source in range(count)]
    return lax.ppermute(value, axis, pairs)


def along(site):
    rows, places = lax.axis_size("x"), lax.axis_size("z")
    row, place = divmod(site % (rows * places), places)
    return row * places + (place if row % 2 == 0 else places - 1 - place)


def reordered(value):
    pairs = [(site, along(site)) for site in range(lax.axis_size(TA))]
    return lax.ppermute(value, TA, pairs)


def shifted_along(value, steps):
    pairs = [(along(site), along(site + steps)) for site in range(lax.axis_size(TA))]
    return lax.ppermute(value, TA, pairs)


def exchanged(value, axis):
    return lax.all_to_all(value, axis, 0, 0, tiled=True)


def gathered(value, axis):
    count = lax.axis_size(axis)
    sent = jnp.broadcast_to(value[None], (count,) + value.shape)
    return exchanged(sent, axis)


def dot(left, right):
    return jnp.dot(left, right, precision=HIGHEST, preferred_element_type=jnp.float32)


def dot_t(left, right):
    return lax.dot_general(
        left,
        right,
        (((1,), (1,)), ((), ())),
        precision=HIGHEST,
        preferred_element_type=jnp.float32,
    )


def lower_inverse(matrix):
    size = matrix.shape[0]
    lane = lax.broadcasted_iota(jnp.int32, (TILE, size), 1)
    sublane = lax.broadcasted_iota(jnp.int32, (TILE, size), 0)
    groups = [matrix[g * TILE : (g + 1) * TILE, :] for g in range(size // TILE)]
    full = (TILE, size)
    for pivot in range(size):
        own, inner = divmod(pivot, TILE)
        row = jnp.broadcast_to(groups[own][inner : inner + 1, :], full)
        columns = {
            g: jnp.broadcast_to(groups[g][:, pivot : pivot + 1], full)
            for g in range(own, len(groups))
        }
        scale = 1.0 / jnp.broadcast_to(columns[own][inner : inner + 1, :], full)
        here = lane == pivot
        for g in range(own, len(groups)):
            factors = columns[g] * scale
            updated = jnp.where(here, -factors, groups[g] - factors * row)
            if g == own:
                updated = jnp.where(sublane > inner, updated, groups[g])
            groups[g] = updated
    result = []
    for g in range(len(groups)):
        rows = sublane + g * TILE
        diagonal = jnp.sum(jnp.where(lane == rows, groups[g], 0.0), axis=1, keepdims=True)
        unit = jnp.where(lane < rows, groups[g], jnp.where(lane == rows, 1.0, 0.0))
        result.append(unit * lax.rsqrt(diagonal))
    return jnp.concatenate(result, axis=0)


def split(value):
    high = value.astype(jnp.bfloat16)
    return high, (value - high.astype(jnp.float32)).astype(jnp.bfloat16)


def dot3(left, right, contract):
    dims = (((1,), (contract,)), ((), ()))
    (lh, ll), (rh, rl) = left, right
    one = functools.partial(
        lax.dot_general, dimension_numbers=dims, preferred_element_type=jnp.float32
    )
    return one(lh, rh) + (one(lh, rl) + one(ll, rh))


def select_kernel(scale, selected_ref, gram_ref, filtered_ref, out_ref, root_ref, picked_ref):
    size = root_ref.shape[0]
    half = size // 2
    first_block = gram_ref[0:half, :]
    cross_block = gram_ref[half : 2 * half, :]
    second_block = gram_ref[2 * half : 3 * half, :]
    gram = jnp.concatenate(
        [
            jnp.concatenate([first_block, cross_block.T], axis=1),
            jnp.concatenate([cross_block, second_block], axis=1),
        ],
        axis=0,
    )
    row = lax.broadcasted_iota(jnp.int32, gram.shape, 0)
    column = lax.broadcasted_iota(jnp.int32, gram.shape, 1)
    diagonal = jnp.where(row == column, gram, 0.0)
    across = lax.rsqrt(jnp.sum(diagonal, axis=0, keepdims=True))
    down = lax.rsqrt(jnp.sum(diagonal, axis=1, keepdims=True))
    scaled = gram * down * across
    scaled_parts = split(scaled)
    identity = jnp.where(row == column, 1.0, 0.0)
    root_ref[...] = jnp.where(row > column, -scaled, identity)

    def refine(state):
        step, _ = state
        root = split(root_ref[...])
        half_way = split(dot3(root, scaled_parts, 0))
        residual = dot3(half_way, root, 1) - identity
        lower = jnp.where(row > column, residual, 0.5 * identity * residual)
        root_ref[...] = root_ref[...] - dot3(split(lower), root, 0)
        return step + 1, jnp.sum(residual * residual)

    def unfinished(state):
        step, error = state
        return jnp.logical_and(step < REFINE_STEPS, error >= REFINE_ERROR)

    _, error = lax.while_loop(unfinished, refine, (jnp.int32(0), jnp.float32(1.0)))
    refined = error < REFINE_ERROR

    @pl.when(refined)
    def _():
        root_ref[...] = root_ref[...] * across

    @pl.when(jnp.logical_not(refined))
    def _():
        first = lower_inverse(gram_ref[0:half, :])
        below = dot_t(gram_ref[half : 2 * half, :], first)
        second = lower_inverse(gram_ref[2 * half : 3 * half, :] - dot_t(below, below))
        root_ref[0:half, 0:half] = first
        root_ref[0:half, half:size] = jnp.zeros((half, half), jnp.float32)
        root_ref[half:size, 0:half] = -dot(second, dot(below, first))
        root_ref[half:size, half:size] = second

    count = picked_ref.shape[0]
    for k in range(count):
        picked_ref[k : k + 1, :] = root_ref[pl.ds(selected_ref[k], 1), :]
    coefficients = dot(picked_ref[...] * scale, filtered_ref[...].astype(jnp.float32))
    coefficients = coefficients.astype(jnp.bfloat16).astype(jnp.float32)
    width = coefficients.shape[1]
    lane = lax.broadcasted_iota(jnp.int32, coefficients.shape, 1)
    out_ref[0:count, :] = jnp.where(lane < width // 2, coefficients, -coefficients).astype(
        jnp.bfloat16
    )
    swapped = jnp.concatenate(
        [coefficients[:, width // 2 :], coefficients[:, : width // 2]], axis=1
    )
    out_ref[count : 2 * count, :] = swapped.astype(jnp.bfloat16)


def rebuild_rows(selected, gram, filtered, scale):
    count = selected.shape[0]
    size, width = filtered.shape
    vmem = pl.BlockSpec(memory_space=pltpu.VMEM)
    return pl.pallas_call(
        functools.partial(select_kernel, scale),
        out_shape=jax.ShapeDtypeStruct((2 * count, width), jnp.bfloat16),
        in_specs=[pl.BlockSpec(memory_space=pltpu.SMEM), vmem, vmem],
        out_specs=vmem,
        scratch_shapes=[
            pltpu.VMEM((size, size), jnp.float32),
            pltpu.VMEM((count, size), jnp.float32),
        ],
        compiler_params=pltpu.CompilerParams(vmem_limit_bytes=16 * 2**20),
    )(selected, gram, filtered)


def gram_sum(gram, aside):
    half = gram.shape[0] // 2
    packed = jnp.concatenate([gram[:half, :half], gram[half:, :half], gram[half:, half:]], axis=0)
    depth = lax.axis_size(GZ)
    share = exchanged(packed.reshape(depth, packed.shape[0] // depth, half), GZ).sum(axis=0)
    share = gathered(share, "z").sum(axis=0)
    share, aside = lax.optimization_barrier((share, aside))
    share = gathered(share, "x").sum(axis=0)
    return gathered(share, GZ).reshape(packed.shape), aside


def packed_symmetric(matrix):
    high = lax.reduce_precision(matrix, 8, 7)
    low = matrix - high
    row = lax.broadcasted_iota(jnp.int32, matrix.shape, 0)
    column = lax.broadcasted_iota(jnp.int32, matrix.shape, 1)
    square = jnp.where(row >= column, high, low)
    rest = jnp.sum(jnp.where(row == column, low, 0.0), axis=0, keepdims=True)
    rest = jnp.broadcast_to(rest, (REST_ROWS, rest.shape[1]))
    return jnp.concatenate([square, rest], axis=0).astype(jnp.bfloat16)


def unpacked_symmetric(rows):
    rows = rows.astype(jnp.float32)
    size = rows.shape[1]
    square, rest = rows[:size], rows[size : size + 1]
    row = lax.broadcasted_iota(jnp.int32, square.shape, 0)
    column = lax.broadcasted_iota(jnp.int32, square.shape, 1)
    return square + jnp.where(row == column, rest, square.T)


def local(coarse_vectors, self_links, hop_links, basis, selected):
    sent = reordered(coarse_vectors[0, 0, 0, 0].astype(jnp.bfloat16))
    hops = hop_links[:, 0, 0, 0, 0]
    hop_x = hops[0].astype(jnp.float32)
    hop_y = hops[1].astype(jnp.float32)
    site = self_links[0, 0, 0, 0].astype(jnp.float32) + (hop_x + hop_x.T) + (hop_y + hop_y.T)
    width = site.shape[0]
    own = reordered(jnp.concatenate([hops[2], hops[3], packed_symmetric(site)], axis=0))
    above_z, above_t = own[:width], own[width : 2 * width]
    site = unpacked_symmetric(own[2 * width :])
    start = sent.astype(jnp.float32)

    def halos(down_t, up_t, up_z, down_z):
        from_below_t = shifted_along(up_t, 1)
        from_above_t = shifted_along(down_t, -1)
        from_below_z = shifted(up_z, GZ, 1)
        from_above_z = shifted(down_z, GZ, -1)
        return from_below_t, from_above_t, from_below_z, from_above_z

    def product(halo, links):
        halo = jnp.concatenate(halo, axis=1)
        return jnp.dot(halo, links, preferred_element_type=jnp.float32)

    up_t = jnp.concatenate([sent, above_t.T], axis=0)
    up_z = jnp.concatenate([sent, above_z.T], axis=0)
    count = sent.shape[0]
    near_t, far_t, near_z, far_z = halos(sent, up_t, up_z, sent)
    around = jnp.concatenate([near_t[count:], above_t, near_z[count:], above_z], axis=0)
    halo = near_t[:count], far_t, near_z[:count], far_z

    earlier = start
    current = dot(start, site) + product(halo, around)
    site2 = 2.0 * site
    around2 = 2.0 * around
    for _ in range(DEG - 1):
        near = dot(current, site2) - earlier
        sent = current.astype(jnp.bfloat16)
        halo = halos(sent, sent, sent, sent)
        earlier, current = current, near + product(halo, around2)
    gram, filtered = gram_sum(dot_t(current, current), reordered(current.astype(jnp.bfloat16)))
    total = lax.axis_size(GZ) * lax.axis_size(TA) * start.shape[1]
    count = selected.shape[0]
    stacked = rebuild_rows(selected, gram, filtered, float(total) ** 0.5)
    rebuilt = jnp.dot(stacked, basis[0, 0, 0, 0], preferred_element_type=jnp.float32)
    return rebuilt.astype(jnp.bfloat16).reshape(1, 1, 1, 1, 2, count, basis.shape[-1])


def solution(mesh):
    fine = Mesh(mesh.devices.reshape(8, 2, 4, 12), ("y", "c", "x", "z"))
    in_specs = (
        P(GZ, TA, None, None, None, None),
        P(GZ, TA, None, None, None, None),
        P(None, GZ, TA, None, None, None, None),
        P(GZ, TA, None, None, None, None),
        P(),
    )
    out_specs = P(GZ, TA, None, None, None, None, None)
    return jax.shard_map(local, mesh=fine, in_specs=in_specs, out_specs=out_specs, check_vma=False)
```
